256 devices in a mesh: seg: 4 (over z_hi, core), space: 64 (over y, x, z_lo).
Axes of the slice: x: 4, y: 4, z: 8 (z_hi: 2, z_lo: 4; z = z_hi * 4 + z_lo), core: 2. Of those that a mesh axis runs over, the one named last changes fastest.
Arguments:
- directions: float32 [4, 16, 256, 64, 128], P('seg', None, 'space'), may hold values from -100 to 100
- adjoint: float32 [4, 256, 64, 128], P('seg', 'space'), may hold values from -1000 to 1000
- velocity: float32 [4, 3, 256, 64, 128], P('seg', None, 'space'), may hold values from -1 to 1
- diffusivity: float32 [4, 256, 64, 128], P('seg', 'space'), may hold values from 0.05 to 0.15
- objective_source: float32 [4, 256, 64, 128], P('seg', 'space'), may hold values from -6 to 6
- segment_start: int32 [4], P('seg'), may hold values from 0 to 999
Outputs:
- basis_rows: float32 [4, 16, 256, 64, 128], P('seg', None, 'space')
- factor_upper: float32 [4, 16, 16], P('seg')
- coefficients: float32 [4, 16], P('seg')
- shadow: float32 [4, 256, 64, 128], P('seg', 'space')
- gradient: float32 [256, 64, 128], P('space', 'seg')
The draws below stay inside these ranges and needn't reach their ends.
All inputs are finite; a program needn't handle non-finite values.
Results may differ from the reference program's by a relative error of at most 0.0003.
Values sent between devices are 32-bit elements; how exact they have to be, the bound alone decides.
A program may use at most 64 MiB of HBM per device.

```python
import math
import jax
import jax.numpy as jnp
from jax import lax

M = 16
NY = 64
NZ = 128
SEGS = 4
NX = 256


def common_fields(key):
    base = jax.random.fold_in(key, 11)
    noise = jnp.clip(jax.random.normal(jax.random.fold_in(base, 1), (SEGS, M, NX, NY, NZ), jnp.float32), -5.0, 5.0)
    shared = jnp.clip(jax.random.normal(jax.random.fold_in(base, 2), (SEGS, 1, NX, NY, NZ), jnp.float32), -5.0, 5.0)
    mixing = jax.random.uniform(jax.random.fold_in(base, 3), (SEGS, M, 1, 1, 1), jnp.float32, 0.5, 1.0)
    fields = noise + mixing * shared
    weights = jax.random.uniform(jax.random.fold_in(base, 5), (SEGS, M, 1, 1, 1), jnp.float32, -0.6, 0.6)
    lone = jnp.clip(jax.random.normal(jax.random.fold_in(base, 6), (SEGS, NX, NY, NZ), jnp.float32), -5.0, 5.0)
    adjoint_field = lone + jnp.sum(weights * fields, axis=1)
    return (fields, adjoint_field)


def draw_directions(key, part):
    return common_fields(key)[0]


def draw_adjoint(key, part):
    return common_fields(key)[1]


def plant(result, key, smallest, high):
    spot = [jax.random.randint(jax.random.fold_in(key, axis), (), 0, length) for axis, length in enumerate(result.shape)]
    widest = result.shape.index(max(result.shape))
    next_to = spot[:widest] + [(spot[widest] + 1) % result.shape[widest]] + spot[widest + 1:]
    return result.at[tuple(spot)].set(smallest).at[tuple(next_to)].set(high)


def shard_levels(stream_key, dims, split, low, largest):
    loudness, own = 1.0, jax.random.fold_in(stream_key, 6)
    for axis_at, blocks in split:
        heights = jnp.exp(jax.random.uniform(jax.random.fold_in(own, axis_at), (blocks,), jnp.float32, low / len(split), largest / len(split)))
        loudness = loudness * jnp.repeat(heights, dims[axis_at] // blocks).reshape([-1 if axis == axis_at else 1 for axis in range(len(dims))])
    return loudness


def centred(own_key, shape, deviation, most, cuts=(), kind=jnp.bfloat16):
    drawn = deviation * jax.random.normal(own_key, shape, jnp.float32)
    if cuts:
        drawn = drawn * shard_levels(own_key, shape, cuts, -0.22, 0.18)
    return jnp.clip(drawn, -most, most).astype(kind)


def setup_inputs(seed: int = 0) -> dict:
    seeds = jax.random.split(jax.random.key(seed), 7)
    return {
        "directions": draw_directions(jax.random.fold_in(seeds[6], 71), 0),
        "adjoint": draw_adjoint(jax.random.fold_in(seeds[6], 71), 0),
        "velocity": centred(seeds[2], (SEGS, 3, NX, NY, NZ), 0.3, 1.0, ((0, 4), (2, 64)), jnp.float32),
        "diffusivity": jnp.clip(0.05 + 0.10000001 * jax.random.uniform(seeds[3], (SEGS, NX, NY, NZ), jnp.float32) ** shard_levels(seeds[3], (SEGS, NX, NY, NZ), ((0, 4), (1, 64)), -0.2, 0.2), 0.05, 0.15),
        "objective_source": centred(seeds[4], (SEGS, NX, NY, NZ), 1.0, 6.0, ((0, 4), (1, 64)), jnp.float32),
        "segment_start": plant(jax.random.randint(seeds[5], (SEGS,), 0, 1000), jax.random.fold_in(seeds[5], 1), 0, 999).astype(jnp.int32),
    }


def modulation(window_start, section):
    phase_step = (window_start + 2 - section) % 64
    return 1.0 + 0.5 * jnp.sin(2.0 * math.pi * phase_step.astype(jnp.float32) / 64.0)

def advance(stacked, diffusivity, velocity, strength):
    forward_x = jnp.roll(stacked, -1, axis=1)
    behind_x = jnp.roll(stacked, 1, axis=1)
    wall_zero = jnp.zeros_like(stacked[:, :, :1])
    forward_y = jnp.concatenate([stacked[:, :, 1:], wall_zero], axis=2)
    behind_y = jnp.concatenate([wall_zero, stacked[:, :, :-1]], axis=2)
    forward_z = jnp.roll(stacked, -1, axis=3)
    behind_z = jnp.roll(stacked, 1, axis=3)
    laplace = forward_x + behind_x + forward_y + behind_y + forward_z + behind_z - 6.0 * stacked
    transport = velocity[0] * (forward_x - behind_x) + velocity[1] * (forward_y - behind_y) + velocity[2] * (forward_z - behind_z)
    return stacked + diffusivity * laplace + 0.5 * strength * transport

def one_segment(directions, adjoint, velocity, diffusivity, source, window_start):
    stacked = jnp.concatenate([directions, adjoint[None]], axis=0)
    stacked = advance(stacked, diffusivity, velocity, modulation(window_start, 1))
    stacked = stacked.at[-1].add(source)
    first_adjoint = stacked[-1]
    stacked = advance(stacked, diffusivity, velocity, modulation(window_start, 2))
    stacked = stacked.at[-1].add(source)
    flattened = stacked.reshape(M + 1, -1)
    cell_count = NX * NY * NZ
    summed = jnp.dot(flattened[:M], flattened.T, precision=lax.Precision.HIGHEST) / cell_count
    triangle = jnp.linalg.cholesky(summed[:, :M])
    inverse = jax.scipy.linalg.solve_triangular(triangle, jnp.eye(M, dtype=triangle.dtype), lower=True)
    basis_rows = jnp.dot(inverse, flattened[:M], precision=lax.Precision.HIGHEST)
    coefficients = jnp.dot(inverse, summed[:, M], precision=lax.Precision.HIGHEST)
    shadow = flattened[M] - jnp.dot(coefficients, basis_rows, precision=lax.Precision.HIGHEST)
    shadow = shadow.reshape(NX, NY, NZ)
    return (basis_rows.reshape(M, NX, NY, NZ), triangle.T, coefficients, shadow, first_adjoint + shadow)

def reference(directions, adjoint, velocity, diffusivity, objective_source, segment_start):
    basis_all = []
    factor_all = []
    coef_all = []
    shadow_all = []
    gradient = jnp.zeros((NX, NY, NZ), jnp.float32)
    for segment in range(SEGS):
        outputs = one_segment(directions[segment], adjoint[segment], velocity[segment], diffusivity[segment], objective_source[segment], segment_start[segment])
        basis_all.append(outputs[0])
        factor_all.append(outputs[1])
        coef_all.append(outputs[2])
        shadow_all.append(outputs[3])
        gradient = gradient + outputs[4]
    return (jnp.stack(basis_all), jnp.stack(factor_all), jnp.stack(coef_all), jnp.stack(shadow_all), gradient)
```

```python
import functools
import math

import jax
import jax.numpy as jnp
from jax import lax
from jax.experimental import pallas as pl
from jax.experimental.pallas import tpu as pltpu
from jax.sharding import PartitionSpec as P

MESH = pl.DeviceIdType.MESH
DIRS = 16
FIELDS = 17
LAYERS = 4
BLOCKS = 8
POS = LAYERS * BLOCKS
AHEAD = 4
F32 = jnp.float32


def place_of(size):
    depth = min(4, size)
    width = min(4, size // depth)
    height = size // (depth * width)
    return height, width, depth


def peers_of(me, size):
    height, width, depth = place_of(size)
    z = lax.rem(me, depth)
    x = lax.rem(lax.div(me, depth), width)
    y = lax.div(me, depth * width)
    stages = [
        [(y * width + lax.rem(x + d, width)) * depth + z for d in range(1, width)],
        [(lax.rem(y + d, height) * width + x) * depth + z for d in range(1, height)],
        [(y * width + x) * depth + lax.rem(z + d, depth) for d in range(1, depth)],
    ]
    return [stage for stage in stages if stage]


def layer(ref, lead, x):
    return ref[(*lead, pl.ds(BLOCKS * x, BLOCKS))].reshape(BLOCKS * 8, 128)


def stencil(here, ahead, behind, coef, step, x):
    c = [layer(coef, (step, n), x) for n in range(7)]
    out = c[0] * here + c[1] * ahead + c[2] * behind
    out = out + c[3] * pltpu.roll(here, BLOCKS * 8 - 1, 0) + c[4] * pltpu.roll(here, 1, 0)
    return out + c[5] * pltpu.roll(here, 127, 1) + c[6] * pltpu.roll(here, 1, 1)


def kernel(
    size, segs, cells,
    start_ref, dirs_ref, adj_ref, vel_ref, dif_ref, src_ref,
    basis_ref, upper_ref, coef_ref, shadow_ref, grad_ref,
    f_all, g_all, w_all, f_halo, g_halo, coef, vel, dif, src, basis,
    gram, gram_cur, gram_got, along_cur, along_got, columns, inverse_rows, spread, inverse, weights, terms, arrived,
    load_sem, store_sem, f_send, f_recv, g_send, g_recv,
    gram_send, gram_recv, along_send, along_recv, term_send, term_recv,
):
    seg = lax.axis_index("seg")
    me = lax.axis_index("space")
    right, left = lax.rem(me + 1, size), lax.rem(me + size - 1, size)
    stages = peers_of(me, size)

    loads = [
        pltpu.make_async_copy(dirs_ref, f_all.at[pl.ds(0, DIRS)], load_sem.at[0]),
        pltpu.make_async_copy(adj_ref, f_all.at[DIRS], load_sem.at[1]),
        pltpu.make_async_copy(vel_ref, vel, load_sem.at[2]),
        pltpu.make_async_copy(dif_ref, dif, load_sem.at[3]),
        pltpu.make_async_copy(src_ref, src, load_sem.at[4]),
    ]
    for load in loads:
        load.start()

    barrier = pltpu.get_barrier_semaphore()
    greeted = [{"space": left}, {"space": right}]
    greeted += [{"space": peer} for stage in stages for peer in stage]
    greeted += [{"seg": lax.rem(seg + d, segs)} for d in range(1, segs)]
    for device in greeted:
        pl.semaphore_signal(barrier, inc=1, device_id=device, device_id_type=MESH)

    def clear(n, _):
        w_all[n] = jnp.zeros((POS, 8, 128), F32)
        return 0

    lax.fori_loop(0, FIELDS, clear, 0)
    gram[...] = jnp.zeros_like(gram)
    for load in loads:
        load.wait()
    pl.semaphore_wait(barrier, len(greeted))

    def halo(source, landing, send, recv, n, side):
        edge = BLOCKS * (LAYERS - 1) if side == 0 else 0
        return pltpu.make_async_remote_copy(
            source.at[n, pl.ds(edge, BLOCKS)],
            landing.at[side, n],
            send.at[side, n],
            recv.at[side, n],
            device_id={"space": right if side == 0 else left},
            device_id_type=MESH,
        )

    f_copy = functools.partial(halo, f_all, f_halo, f_send, f_recv)
    g_copy = functools.partial(halo, g_all, g_halo, g_send, g_recv)
    for n in range(AHEAD):
        for side in range(2):
            f_copy(n, side).start()

    row = lax.broadcasted_iota(jnp.int32, (BLOCKS * 8, 128), 0)
    for step in range(2):
        phase = jnp.full((8, 128), start_ref[0], jnp.int32) + (1 - step)
        turn = lax.rem(phase, jnp.full((8, 128), 64, jnp.int32)).astype(F32)
        half = 0.5 * (1.0 + 0.5 * jnp.sin(2.0 * math.pi * turn / 64.0))
        half = jnp.broadcast_to(half[0:1], (BLOCKS * 8, 128))

        def prepare(x, _, step=step, half=half):
            spot = pl.ds(BLOCKS * x, BLOCKS)
            d = layer(dif, (), x)
            values = [1.0 - 6.0 * d]
            for axis in range(3):
                drift = half * layer(vel, (axis,), x)
                values += [d + drift, d - drift]
            values[3] = jnp.where(row == BLOCKS * 8 - 1, 0.0, values[3])
            values[4] = jnp.where(row == 0, 0.0, values[4])
            for n in range(7):
                coef[step, n, spot] = values[n].reshape(BLOCKS, 8, 128)
            return 0

        lax.fori_loop(0, LAYERS, prepare, 0)

    def advance(step, source, landing, target, n, layers):
        for x in layers:
            here = layer(source, (n,), x)
            ahead = layer(source, (n,), x + 1) if x < LAYERS - 1 else landing[1, n].reshape(BLOCKS * 8, 128)
            behind = layer(source, (n,), x - 1) if x > 0 else landing[0, n].reshape(BLOCKS * 8, 128)
            out = stencil(here, ahead, behind, coef, step, x)
            target[n, pl.ds(BLOCKS * x, BLOCKS)] = out.reshape(BLOCKS, 8, 128)

        @pl.when(n == DIRS)
        def _():
            for x in layers:
                spot = pl.ds(BLOCKS * x, BLOCKS)
                target[n, spot] = target[n, spot] + src[spot]

    def first(n, _):
        for side in range(2):
            f_copy(n, side).wait_recv()
        advance(0, f_all, f_halo, g_all, n, (0, 3))
        for side in range(2):
            f_copy(n, side).wait_send()

        @pl.when(n + AHEAD < FIELDS)
        def _():
            for side in range(2):
                f_copy(n + AHEAD, side).start()

        @pl.when(n + AHEAD >= FIELDS)
        def _():
            for side in range(2):
                g_copy(n + AHEAD - FIELDS, side).start()

        advance(0, f_all, f_halo, g_all, n, (1, 2))
        return 0

    lax.fori_loop(0, FIELDS, first, 0)

    lane = lax.broadcasted_iota(jnp.int32, (DIRS, 128), 1)

    def products(n):
        def at(p, total):
            return total + w_all[0:DIRS, p] * w_all[n, p][None]

        total = lax.fori_loop(0, POS, at, jnp.zeros((DIRS, 8, 128), F32), unroll=4)
        return jnp.sum(jnp.sum(total, axis=1), axis=1, keepdims=True)

    def second(n):
        advance(1, g_all, g_halo, w_all, n, (1, 2))
        for side in range(2):
            g_copy(n, side).wait_recv()
            g_copy(n, side).wait_send()

        @pl.when(n + AHEAD < FIELDS)
        def _():
            for side in range(2):
                g_copy(n + AHEAD, side).start()

        advance(1, g_all, g_halo, w_all, n, (0, 3))
        return products(n)

    def gram_row(n, _):
        gram[...] = jnp.where(lane == n, second(n), gram[...])
        return 0

    lax.fori_loop(0, DIRS, gram_row, 0)

    def exchange(cur, got, send, recv, k):
        base = sum(len(stage) for stage in stages[:k])
        return [
            pltpu.make_async_remote_copy(
                cur.at[k], got.at[base + n], send.at[base + n], recv.at[base + n],
                device_id={"space": peer}, device_id_type=MESH,
            )
            for n, peer in enumerate(stages[k])
        ]

    gram_parts = functools.partial(exchange, gram_cur, gram_got, gram_send, gram_recv)
    along_parts = functools.partial(exchange, along_cur, along_got, along_send, along_recv)

    def collect(parts, cur, got, k):
        base = sum(len(stage) for stage in stages[:k])
        for copy in parts(k):
            copy.wait_recv()
        total = cur[k]
        for n in range(len(stages[k])):
            total = total + got[base + n]
        cur[k + 1] = total

    gram_cur[0] = gram[...]
    for copy in gram_parts(0):
        copy.start()
    along_cur[0] = jnp.broadcast_to(second(DIRS), (DIRS, 128))
    for copy in along_parts(0):
        copy.start()
    count = len(stages)
    for k in range(count):
        collect(gram_parts, gram_cur, gram_got, k)
        if k + 1 < count:
            for copy in gram_parts(k + 1):
                copy.start()
            collect(along_parts, along_cur, along_got, k)
            for copy in along_parts(k + 1):
                copy.start()

    whole = gram_cur[count] * (1.0 / cells)
    for j in range(DIRS):
        columns[j] = jnp.broadcast_to(whole[:, j:j + 1], (DIRS, 128))
    lane8 = lax.broadcasted_iota(jnp.int32, (8, 128), 1)
    cols = [jnp.broadcast_to(columns[k:DIRS, k:k + 1, :], (DIRS - k, 8, 128)) for k in range(DIRS)]
    rows = [
        jnp.broadcast_to(whole[i:i + 1], (8, 128)) + jnp.where(lane8 == 32 + i, 1.0, 0.0) for i in range(DIRS)
    ]
    for k in range(DIRS):
        scale = lax.rsqrt(cols[k][0])
        lower = cols[k] * scale[None]
        done = rows[k] * scale
        inverse_rows[k:k + 1, :] = done[0:1]
        for j in range(k + 1, DIRS):
            cols[j] = cols[j] - lower[j - k:] * lower[j - k][None]
            rows[j] = rows[j] - lower[j - k] * done
    solved = inverse_rows[...]
    for k in range(DIRS):
        spread[k] = jnp.broadcast_to(solved[:, 32 + k:33 + k], (DIRS, 128))

    collect(along_parts, along_cur, along_got, count - 1)
    along = along_cur[count] * (1.0 / cells)
    found = spread[0] * jnp.broadcast_to(along[0:1], (DIRS, 128))
    for k in range(1, DIRS):
        found = found + spread[k] * jnp.broadcast_to(along[k:k + 1], (DIRS, 128))
    for k in range(DIRS):
        weights[k] = jnp.broadcast_to(jnp.sum(spread[k] * found, axis=0, keepdims=True), (8, 128))

    def piece(t, _):
        for x in range(LAYERS):
            for h in range(2):
                p = BLOCKS * x + 2 * t + h
                value = w_all[DIRS, p]
                for k in range(DIRS):
                    value = value - weights[k] * w_all[k, p]
                shadow_ref[p] = value
                terms[t, 2 * x + h] = value + g_all[DIRS, p]
        return 0

    lax.fori_loop(0, segs, piece, 0)
    term_copies = [
        pltpu.make_async_remote_copy(
            terms.at[lax.rem(seg + d, segs)], arrived.at[d - 1], term_send.at[d - 1], term_recv.at[d - 1],
            device_id={"seg": lax.rem(seg + d, segs)}, device_id_type=MESH,
        )
        for d in range(1, segs)
    ]
    for copy in term_copies:
        copy.start()

    upper_ref[...] = jnp.where(lane >= lax.broadcasted_iota(jnp.int32, (DIRS, 128), 0), solved, 0.0)[:, 0:DIRS]
    diagonal = lane == lax.broadcasted_iota(jnp.int32, (DIRS, 128), 0)
    coef_ref[...] = jnp.sum(jnp.where(diagonal, found, 0.0), axis=0, keepdims=True)[:, 0:DIRS]

    for k in range(DIRS):
        for i in range(k, DIRS):
            inverse[i, k] = jnp.broadcast_to(spread[k, i:i + 1, :], (8, 128))

    def rows_at(q, _):
        spot = pl.ds(2 * q, 2)
        values = [w_all[k, spot] for k in range(DIRS)]
        for i in range(DIRS):
            total = inverse[i, 0][None] * values[0]
            for k in range(1, i + 1):
                total = total + inverse[i, k][None] * values[k]
            basis[i, spot] = total
        return 0

    stores = []
    for x in range(LAYERS):
        lax.fori_loop(x * BLOCKS // 2, (x + 1) * BLOCKS // 2, rows_at, 0)
        spot = pl.ds(BLOCKS * x, BLOCKS)
        store = pltpu.make_async_copy(basis.at[:, spot], basis_ref.at[:, spot], store_sem.at[x])
        store.start()
        stores.append(store)

    for copy in term_copies:
        copy.wait_recv()
    grad_ref[...] = terms[seg] + arrived[0] + arrived[1] + arrived[2]
    for copy in term_copies:
        copy.wait_send()
    for k in range(count):
        for copy in gram_parts(k) + along_parts(k):
            copy.wait_send()
    for store in stores:
        store.wait()


def body(directions, adjoint, velocity, diffusivity, objective_source, segment_start):
    size, segs = lax.axis_size("space"), lax.axis_size("seg")
    tile = (POS, 8, 128)
    cells = POS * 8 * 128 * size
    peers = sum(n - 1 for n in place_of(size))
    count = sum(n > 1 for n in place_of(size))
    hbm, vmem = pl.BlockSpec(memory_space=pl.ANY), pl.BlockSpec(memory_space=pltpu.VMEM)
    dma = pltpu.SemaphoreType.DMA
    outs = pl.pallas_call(
        functools.partial(kernel, size, segs, cells),
        out_shape=(
            jax.ShapeDtypeStruct((DIRS, *tile), F32),
            jax.ShapeDtypeStruct((DIRS, DIRS), F32),
            jax.ShapeDtypeStruct((1, DIRS), F32),
            jax.ShapeDtypeStruct(tile, F32),
            jax.ShapeDtypeStruct((2 * LAYERS, 8, 128), F32),
        ),
        in_specs=[pl.BlockSpec(memory_space=pltpu.SMEM)] + [hbm] * 5,
        out_specs=(hbm, vmem, vmem, vmem, vmem),
        scratch_shapes=[
            pltpu.VMEM((FIELDS, *tile), F32),
            pltpu.VMEM((FIELDS, *tile), F32),
            pltpu.VMEM((FIELDS, *tile), F32),
            pltpu.VMEM((2, FIELDS, BLOCKS, 8, 128), F32),
            pltpu.VMEM((2, FIELDS, BLOCKS, 8, 128), F32),
            pltpu.VMEM((2, 7, *tile), F32),
            pltpu.VMEM((3, *tile), F32),
            pltpu.VMEM(tile, F32),
            pltpu.VMEM(tile, F32),
            pltpu.VMEM((DIRS, *tile), F32),
            pltpu.VMEM((DIRS, 128), F32),
            pltpu.VMEM((count + 1, DIRS, 128), F32),
            pltpu.VMEM((peers, DIRS, 128), F32),
            pltpu.VMEM((count + 1, DIRS, 128), F32),
            pltpu.VMEM((peers, DIRS, 128), F32),
            pltpu.VMEM((DIRS, DIRS, 128), F32),
            pltpu.VMEM((DIRS, 128), F32),
            pltpu.VMEM((DIRS, DIRS, 128), F32),
            pltpu.VMEM((DIRS, DIRS, 8, 128), F32),
            pltpu.VMEM((DIRS, 8, 128), F32),
            pltpu.VMEM((4, 2 * LAYERS, 8, 128), F32),
            pltpu.VMEM((3, 2 * LAYERS, 8, 128), F32),
            dma((5,)), dma((LAYERS,)),
            dma((2, FIELDS)), dma((2, FIELDS)), dma((2, FIELDS)), dma((2, FIELDS)),
            dma((peers,)), dma((peers,)), dma((peers,)), dma((peers,)),
            dma((3,)), dma((3,)),
        ],
        compiler_params=pltpu.CompilerParams(
            collective_id=0, has_side_effects=True, vmem_limit_bytes=40 * 1024 * 1024
        ),
        cost_estimate=pl.CostEstimate(flops=120_000_000, bytes_accessed=5_200_000, transcendentals=64),
        name="shadowing",
    )(
        segment_start,
        directions.reshape(DIRS, *tile),
        adjoint.reshape(tile),
        velocity.reshape(3, *tile),
        diffusivity.reshape(tile),
        objective_source.reshape(tile),
    )
    basis_rows, upper, coefficients, shadow, gradient = outs
    return (
        basis_rows.reshape(directions.shape),
        upper[None],
        coefficients,
        shadow.reshape(adjoint.shape),
        gradient.reshape(LAYERS, 16, 128),
    )


def solution(mesh):
    return jax.shard_map(
        body,
        mesh=mesh,
        in_specs=(
            P("seg", None, "space", None, None),
            P("seg", "space", None, None),
            P("seg", None, "space", None, None),
            P("seg", "space", None, None),
            P("seg", "space", None, None),
            P("seg"),
        ),
        out_specs=(
            P("seg", None, "space", None, None),
            P("seg", None, None),
            P("seg", None),
            P("seg", "space", None, None),
            P("space", "seg", None),
        ),
        check_vma=False,
    )
```

```python
import functools
import math

import jax
import jax.numpy as jnp
from jax import lax
from jax.experimental import pallas as pl
from jax.experimental.pallas import tpu as pltpu
from jax.sharding import PartitionSpec as P

MESH = pl.DeviceIdType.MESH
DIRS = 16
FIELDS = 17
LAYERS = 4
BLOCKS = 8
POS = LAYERS * BLOCKS
F32 = jnp.float32


def place_of(size):
    depth = min(4, size)
    width = min(4, size // depth)
    height = size // (depth * width)
    return height, width, depth


def peers_of(me, size):
    height, width, depth = place_of(size)
    z = lax.rem(me, depth)
    x = lax.rem(lax.div(me, depth), width)
    y = lax.div(me, depth * width)
    stages = [
        [
            (lax.rem(y + a, height) * width + lax.rem(x + b, width)) * depth + z
            for a in range(height) for b in range(width) if a or b
        ],
        [(y * width + x) * depth + lax.rem(z + d, depth) for d in range(1, depth)],
    ]
    return [stage for stage in stages if stage]


def layer(ref, lead, x):
    return ref[(*lead, pl.ds(BLOCKS * x, BLOCKS))].reshape(BLOCKS * 8, 128)


def stencil(here, ahead, behind, coef, step, x):
    c = [layer(coef, (step, n), x) for n in range(7)]
    out = c[0] * here + c[1] * ahead + c[2] * behind
    out = out + c[3] * pltpu.roll(here, BLOCKS * 8 - 1, 0) + c[4] * pltpu.roll(here, 1, 0)
    return out + c[5] * pltpu.roll(here, 127, 1) + c[6] * pltpu.roll(here, 1, 1)


def kernel(
    size, segs, cells,
    start_ref, dirs_ref, adj_ref, vel_ref, dif_ref, src_ref,
    basis_ref, upper_ref, coef_ref, shadow_ref, grad_ref,
    f_all, g_all, w_all, f_halo, g_halo, coef, vel, dif, src,
    gram, gram_cur, gram_got, along_cur, along_got, columns, inverse_rows, spread, inverse, weights, terms, arrived,
    load_sem, f_send, f_recv, g_send, g_recv,
    gram_send, gram_recv, along_send, along_recv, term_send, term_recv,
):
    seg = lax.axis_index("seg")
    me = lax.axis_index("space")
    right, left = lax.rem(me + 1, size), lax.rem(me + size - 1, size)
    stages = peers_of(me, size)

    loads = [
        pltpu.make_async_copy(dirs_ref, f_all.at[pl.ds(0, DIRS)], load_sem.at[0]),
        pltpu.make_async_copy(adj_ref, f_all.at[DIRS], load_sem.at[1]),
        pltpu.make_async_copy(vel_ref, vel, load_sem.at[2]),
        pltpu.make_async_copy(dif_ref, dif, load_sem.at[3]),
        pltpu.make_async_copy(src_ref, src, load_sem.at[4]),
    ]
    for load in loads:
        load.start()

    barrier = pltpu.get_barrier_semaphore()
    greeted = [{"space": left}, {"space": right}]
    greeted += [{"space": peer} for stage in stages for peer in stage]
    greeted += [{"seg": lax.rem(seg + d, segs)} for d in range(1, segs)]
    for device in greeted:
        pl.semaphore_signal(barrier, inc=1, device_id=device, device_id_type=MESH)

    def clear(n, _):
        w_all[n] = jnp.zeros((POS, 8, 128), F32)
        return 0

    lax.fori_loop(0, FIELDS, clear, 0)
    gram[...] = jnp.zeros_like(gram)
    pl.semaphore_wait(barrier, len(greeted))

    def halo(source, landing, send, recv, n, side):
        return pltpu.make_async_remote_copy(
            source,
            landing.at[side, n],
            send.at[side, n],
            recv.at[side, n],
            device_id={"space": right if side == 0 else left},
            device_id_type=MESH,
        )

    edges = (pl.ds(BLOCKS * (LAYERS - 1), BLOCKS), pl.ds(0, BLOCKS))

    def f_copy(n, side):
        source = adj_ref.at[edges[side]] if n is DIRS else dirs_ref.at[n, edges[side]]
        return halo(source, f_halo, f_send, f_recv, n, side)

    def g_copy(n, side):
        return halo(g_all.at[n, edges[side]], g_halo, g_send, g_recv, n, side)

    def begin(n, _):
        for side in range(2):
            f_copy(n, side).start()
        return 0

    lax.fori_loop(0, DIRS, begin, 0)
    begin(DIRS, 0)

    for load in loads:
        load.wait()
    row = lax.broadcasted_iota(jnp.int32, (BLOCKS * 8, 128), 0)
    for step in range(2):
        phase = jnp.full((8, 128), start_ref[0], jnp.int32) + (1 - step)
        turn = lax.rem(phase, jnp.full((8, 128), 64, jnp.int32)).astype(F32)
        half = 0.5 * (1.0 + 0.5 * jnp.sin(2.0 * math.pi * turn / 64.0))
        half = jnp.broadcast_to(half[0:1], (BLOCKS * 8, 128))

        def prepare(x, _, step=step, half=half):
            spot = pl.ds(BLOCKS * x, BLOCKS)
            d = layer(dif, (), x)
            values = [1.0 - 6.0 * d]
            for axis in range(3):
                drift = half * layer(vel, (axis,), x)
                values += [d + drift, d - drift]
            values[3] = jnp.where(row == BLOCKS * 8 - 1, 0.0, values[3])
            values[4] = jnp.where(row == 0, 0.0, values[4])
            for n in range(7):
                coef[step, n, spot] = values[n].reshape(BLOCKS, 8, 128)
            return 0

        lax.fori_loop(0, LAYERS, prepare, 0)

    def advance(step, source, landing, target, n, layers):
        for x in layers:
            here = layer(source, (n,), x)
            ahead = layer(source, (n,), x + 1) if x < LAYERS - 1 else landing[1, n].reshape(BLOCKS * 8, 128)
            behind = layer(source, (n,), x - 1) if x > 0 else landing[0, n].reshape(BLOCKS * 8, 128)
            out = stencil(here, ahead, behind, coef, step, x)
            if n is DIRS:
                out = out + layer(src, (), x)
            target[n, pl.ds(BLOCKS * x, BLOCKS)] = out.reshape(BLOCKS, 8, 128)

    def first(n, _):
        for side in range(2):
            f_copy(n, side).wait_recv()
        advance(0, f_all, f_halo, g_all, n, (0, 3))
        for side in range(2):
            g_copy(n, side).start()
        advance(0, f_all, f_halo, g_all, n, (1, 2))
        return 0

    lax.fori_loop(0, DIRS, first, 0)
    first(DIRS, 0)

    lane = lax.broadcasted_iota(jnp.int32, (DIRS, 128), 1)

    def products(n, low, total):
        def at(p, total):
            return total + w_all[0:DIRS, p] * w_all[n, p][None]

        return lax.fori_loop(low, low + BLOCKS, at, total, unroll=4)

    def second(n):
        advance(1, g_all, g_halo, w_all, n, (1, 2))
        total = jnp.zeros((DIRS, 8, 128), F32)
        for x in (1, 2):
            total = products(n, BLOCKS * x, total)
        for side in range(2):
            g_copy(n, side).wait_recv()
        advance(1, g_all, g_halo, w_all, n, (0, 3))
        for x in (0, 3):
            total = products(n, BLOCKS * x, total)
        return jnp.sum(jnp.sum(total, axis=1), axis=1, keepdims=True)

    def gram_row(n, _):
        gram[...] = jnp.where(lane == n, second(n), gram[...])
        return 0

    lax.fori_loop(0, DIRS, gram_row, 0)

    def exchange(cur, got, send, recv, k):
        base = sum(len(stage) for stage in stages[:k])
        return [
            pltpu.make_async_remote_copy(
                cur.at[k], got.at[base + n], send.at[base + n], recv.at[base + n],
                device_id={"space": peer}, device_id_type=MESH,
            )
            for n, peer in enumerate(stages[k])
        ]

    gram_parts = functools.partial(exchange, gram_cur, gram_got, gram_send, gram_recv)
    along_parts = functools.partial(exchange, along_cur, along_got, along_send, along_recv)

    def collect(parts, cur, got, k):
        base = sum(len(stage) for stage in stages[:k])
        for copy in parts(k):
            copy.wait_recv()
        total = cur[k]
        for n in range(len(stages[k])):
            total = total + got[base + n]
        cur[k + 1] = total

    gram_cur[0] = gram[...]
    for copy in gram_parts(0):
        copy.start()
    along_cur[0] = jnp.broadcast_to(second(DIRS), (DIRS, 128))
    for copy in along_parts(0):
        copy.start()
    count = len(stages)
    for k in range(count):
        collect(gram_parts, gram_cur, gram_got, k)
        if k + 1 < count:
            for copy in gram_parts(k + 1):
                copy.start()
            collect(along_parts, along_cur, along_got, k)
            for copy in along_parts(k + 1):
                copy.start()

    whole = gram_cur[count] * (1.0 / cells)
    for j in range(DIRS):
        columns[j] = jnp.broadcast_to(whole[:, j:j + 1], (DIRS, 128))
    lane8 = lax.broadcasted_iota(jnp.int32, (8, 128), 1)
    cols = [jnp.broadcast_to(columns[k:DIRS, k:k + 1, :], (DIRS - k, 8, 128)) for k in range(DIRS)]
    rows = [
        jnp.broadcast_to(whole[i:i + 1], (8, 128)) + jnp.where(lane8 == 32 + i, 1.0, 0.0) for i in range(DIRS)
    ]
    for k in range(DIRS):
        scale = lax.rsqrt(cols[k][0])
        lower = cols[k] * scale[None]
        done = rows[k] * scale
        inverse_rows[k:k + 1, :] = done[0:1]
        for j in range(k + 1, DIRS):
            cols[j] = cols[j] - lower[j - k:] * lower[j - k][None]
            rows[j] = rows[j] - lower[j - k] * done
    solved = inverse_rows[...]
    for k in range(DIRS):
        spread[k] = jnp.broadcast_to(solved[:, 32 + k:33 + k], (DIRS, 128))

    collect(along_parts, along_cur, along_got, count - 1)
    along = along_cur[count] * (1.0 / cells)
    found = spread[0] * jnp.broadcast_to(along[0:1], (DIRS, 128))
    for k in range(1, DIRS):
        found = found + spread[k] * jnp.broadcast_to(along[k:k + 1], (DIRS, 128))
    for k in range(DIRS):
        weights[k] = jnp.broadcast_to(jnp.sum(spread[k] * found, axis=0, keepdims=True), (8, 128))

    def piece(t, _):
        for x in range(LAYERS):
            for h in range(2):
                p = BLOCKS * x + 2 * t + h
                value = w_all[DIRS, p]
                for k in range(DIRS):
                    value = value - weights[k] * w_all[k, p]
                shadow_ref[p] = value
                terms[t, 2 * x + h] = value + g_all[DIRS, p]
        return 0

    lax.fori_loop(0, segs, piece, 0)
    term_copies = [
        pltpu.make_async_remote_copy(
            terms.at[lax.rem(seg + d, segs)], arrived.at[d - 1], term_send.at[d - 1], term_recv.at[d - 1],
            device_id={"seg": lax.rem(seg + d, segs)}, device_id_type=MESH,
        )
        for d in range(1, segs)
    ]
    for copy in term_copies:
        copy.start()

    upper_ref[...] = jnp.where(lane >= lax.broadcasted_iota(jnp.int32, (DIRS, 128), 0), solved, 0.0)[:, 0:DIRS]
    diagonal = lane == lax.broadcasted_iota(jnp.int32, (DIRS, 128), 0)
    coef_ref[...] = jnp.sum(jnp.where(diagonal, found, 0.0), axis=0, keepdims=True)[:, 0:DIRS]

    for k in range(DIRS):
        for i in range(k, DIRS):
            inverse[i, k] = jnp.broadcast_to(spread[k, i:i + 1, :], (8, 128))

    def rows_at(q, _):
        spot = pl.ds(2 * q, 2)
        values = [w_all[k, spot] for k in range(DIRS)]
        for i in range(DIRS):
            total = inverse[i, 0][None] * values[0]
            for k in range(1, i + 1):
                total = total + inverse[i, k][None] * values[k]
            basis_ref[i, spot] = total
        return 0

    lax.fori_loop(0, POS // 2, rows_at, 0)

    for copy in term_copies:
        copy.wait_recv()
    grad_ref[...] = terms[seg] + arrived[0] + arrived[1] + arrived[2]
    for copy in term_copies:
        copy.wait_send()
    for k in range(count):
        for copy in gram_parts(k) + along_parts(k):
            copy.wait_send()

    def sent(n, _):
        for side in range(2):
            f_copy(n, side).wait_send()
            g_copy(n, side).wait_send()
        return 0

    lax.fori_loop(0, DIRS, sent, 0)
    sent(DIRS, 0)


def in_hbm(array):
    return pltpu.with_memory_space_constraint(array, pltpu.HBM)


def in_vmem(array):
    return pltpu.with_memory_space_constraint(array, pltpu.VMEM)


def store_kernel(*refs):
    held, out, sems = refs[:5], refs[5:10], refs[10]
    copies = [pltpu.make_async_copy(held[n], out[n], sems.at[n]) for n in range(5)]
    for copy in copies:
        copy.start()
    for copy in copies:
        copy.wait()


def body(directions, adjoint, velocity, diffusivity, objective_source, segment_start):
    size, segs = lax.axis_size("space"), lax.axis_size("seg")
    tile = (POS, 8, 128)
    cells = POS * 8 * 128 * size
    height, width, depth = place_of(size)
    groups = [n for n in (height * width, depth) if n > 1]
    peers, count = sum(groups) - len(groups), len(groups)
    hbm, vmem = pl.BlockSpec(memory_space=pltpu.HBM), pl.BlockSpec(memory_space=pltpu.VMEM)
    dma = pltpu.SemaphoreType.DMA
    shapes = (
        jax.ShapeDtypeStruct((DIRS, *tile), F32),
        jax.ShapeDtypeStruct((DIRS, DIRS), F32),
        jax.ShapeDtypeStruct((1, DIRS), F32),
        jax.ShapeDtypeStruct(tile, F32),
        jax.ShapeDtypeStruct((2 * LAYERS, 8, 128), F32),
    )
    outs = pl.pallas_call(
        functools.partial(kernel, size, segs, cells),
        out_shape=tuple(pltpu.VMEM(s.shape, F32) for s in shapes),
        in_specs=[pl.BlockSpec(memory_space=pltpu.SMEM)] + [hbm] * 5,
        out_specs=(vmem,) * 5,
        scratch_shapes=[
            pltpu.VMEM((FIELDS, *tile), F32),
            pltpu.VMEM((FIELDS, *tile), F32),
            pltpu.VMEM((FIELDS, *tile), F32),
            pltpu.VMEM((2, FIELDS, BLOCKS, 8, 128), F32),
            pltpu.VMEM((2, FIELDS, BLOCKS, 8, 128), F32),
            pltpu.VMEM((2, 7, *tile), F32),
            pltpu.VMEM((3, *tile), F32),
            pltpu.VMEM(tile, F32),
            pltpu.VMEM(tile, F32),
            pltpu.VMEM((DIRS, 128), F32),
            pltpu.VMEM((count + 1, DIRS, 128), F32),
            pltpu.VMEM((peers, DIRS, 128), F32),
            pltpu.VMEM((count + 1, DIRS, 128), F32),
            pltpu.VMEM((peers, DIRS, 128), F32),
            pltpu.VMEM((DIRS, DIRS, 128), F32),
            pltpu.VMEM((DIRS, 128), F32),
            pltpu.VMEM((DIRS, DIRS, 128), F32),
            pltpu.VMEM((DIRS, DIRS, 8, 128), F32),
            pltpu.VMEM((DIRS, 8, 128), F32),
            pltpu.VMEM((4, 2 * LAYERS, 8, 128), F32),
            pltpu.VMEM((3, 2 * LAYERS, 8, 128), F32),
            dma((5,)),
            dma((2, FIELDS)), dma((2, FIELDS)), dma((2, FIELDS)), dma((2, FIELDS)),
            dma((peers,)), dma((peers,)), dma((peers,)), dma((peers,)),
            dma((3,)), dma((3,)),
        ],
        compiler_params=pltpu.CompilerParams(
            collective_id=0, has_side_effects=True, vmem_limit_bytes=40 * 1024 * 1024
        ),
        cost_estimate=pl.CostEstimate(flops=120_000_000, bytes_accessed=5_200_000, transcendentals=64),
        name="shadowing",
    )(
        segment_start,
        in_hbm(directions.reshape(DIRS, *tile)),
        in_hbm(adjoint.reshape(tile)),
        in_hbm(velocity.reshape(3, *tile)),
        in_hbm(diffusivity.reshape(tile)),
        in_hbm(objective_source.reshape(tile)),
    )
    basis_rows, upper, coefficients, shadow, gradient = pl.pallas_call(
        store_kernel,
        out_shape=shapes,
        in_specs=[pl.BlockSpec(memory_space=pl.ANY)] * 5,
        out_specs=(hbm,) * 5,
        scratch_shapes=[dma((5,))],
        compiler_params=pltpu.CompilerParams(vmem_limit_bytes=1024 * 1024),
        name="store",
    )(*map(in_vmem, outs))
    return (
        basis_rows.reshape(directions.shape),
        upper[None],
        coefficients,
        shadow.reshape(adjoint.shape),
        gradient.reshape(LAYERS, 16, 128),
    )


def solution(mesh):
    return jax.shard_map(
        body,
        mesh=mesh,
        in_specs=(
            P("seg", None, "space", None, None),
            P("seg", "space", None, None),
            P("seg", None, "space", None, None),
            P("seg", "space", None, None),
            P("seg", "space", None, None),
            P("seg"),
        ),
        out_specs=(
            P("seg", None, "space", None, None),
            P("seg", None, None),
            P("seg", None),
            P("seg", "space", None, None),
            P("space", "seg", None),
        ),
        check_vma=False,
    )
```

```python
import functools
import math

import jax
import jax.numpy as jnp
from jax import lax
from jax.experimental import pallas as pl
from jax.experimental.pallas import tpu as pltpu
from jax.sharding import PartitionSpec as P

MESH = pl.DeviceIdType.MESH
DIRS = 16
FIELDS = 17
F_SIZE, G_SIZE = 4, 2
F_GROUPS, G_GROUPS = DIRS // F_SIZE, DIRS // G_SIZE
LAYERS = 4
STORES = 1
BLOCKS = 8
POS = LAYERS * BLOCKS
F32 = jnp.float32


def place_of(size):
    depth = min(4, size)
    width = min(4, size // depth)
    height = size // (depth * width)
    return height, width, depth


def peers_of(me, size):
    height, width, depth = place_of(size)
    z = lax.rem(me, depth)
    x = lax.rem(lax.div(me, depth), width)
    y = lax.div(me, depth * width)
    stages = [
        [
            (lax.rem(y + a, height) * width + lax.rem(x + b, width)) * depth + z
            for a in range(height) for b in range(width) if a or b
        ],
        [(y * width + x) * depth + lax.rem(z + d, depth) for d in range(1, depth)],
    ]
    return [stage for stage in stages if stage]


def layer(ref, lead, x):
    return ref[(*lead, pl.ds(BLOCKS * x, BLOCKS))].reshape(BLOCKS * 8, 128)


def stencil(here, ahead, behind, coef, step, x):
    c = [layer(coef, (step, n), x) for n in range(7)]
    out = c[0] * here + c[1] * ahead + c[2] * behind
    out = out + c[3] * pltpu.roll(here, BLOCKS * 8 - 1, 0) + c[4] * pltpu.roll(here, 1, 0)
    return out + c[5] * pltpu.roll(here, 127, 1) + c[6] * pltpu.roll(here, 1, 1)


def kernel(
    size, segs, cells,
    start_ref, dirs_ref, adj_ref, vel_ref, dif_ref, src_ref,
    basis_ref, upper_ref, coef_ref, shadow_ref, grad_ref,
    f_all, g_all, w_all, f_halo, g_halo, coef, vel, dif, src,
    gram, gram_cur, gram_got, along_cur, along_got, columns, inverse_rows, spread, inverse, weights, terms, arrived,
    load_sem, f_send, f_recv, g_send, g_recv,
    gram_send, gram_recv, along_send, along_recv, term_send, term_recv,
):
    seg = lax.axis_index("seg")
    me = lax.axis_index("space")
    right, left = lax.rem(me + 1, size), lax.rem(me + size - 1, size)
    stages = peers_of(me, size)

    loads = [
        pltpu.make_async_copy(dirs_ref, f_all.at[pl.ds(0, DIRS)], load_sem.at[0]),
        pltpu.make_async_copy(adj_ref, f_all.at[DIRS], load_sem.at[1]),
        pltpu.make_async_copy(vel_ref, vel, load_sem.at[2]),
        pltpu.make_async_copy(dif_ref, dif, load_sem.at[3]),
        pltpu.make_async_copy(src_ref, src, load_sem.at[4]),
    ]
    for load in loads:
        load.start()

    barrier = pltpu.get_barrier_semaphore()
    greeted = [{"space": left}, {"space": right}]
    greeted += [{"space": peer} for stage in stages for peer in stage]
    greeted += [{"seg": lax.rem(seg + d, segs)} for d in range(1, segs)]
    for device in greeted:
        pl.semaphore_signal(barrier, inc=1, device_id=device, device_id_type=MESH)

    def clear(n, _):
        w_all[n] = jnp.zeros((POS, 8, 128), F32)
        return 0

    lax.fori_loop(0, FIELDS, clear, 0)
    gram[...] = jnp.zeros_like(gram)
    pl.semaphore_wait(barrier, len(greeted))

    def halo(source, landing, send, recv, n, side):
        return pltpu.make_async_remote_copy(
            source,
            landing,
            send.at[side, n],
            recv.at[side, n],
            device_id={"space": right if side == 0 else left},
            device_id_type=MESH,
        )

    edges = (pl.ds(BLOCKS * (LAYERS - 1), BLOCKS), pl.ds(0, BLOCKS))

    def f_copy(n, side):
        if n is F_GROUPS:
            return halo(adj_ref.at[edges[side]], f_halo.at[side, DIRS], f_send, f_recv, n, side)
        fields = pl.ds(F_SIZE * n, F_SIZE)
        return halo(dirs_ref.at[fields, edges[side]], f_halo.at[side, fields], f_send, f_recv, n, side)

    def g_copy(n, side):
        fields = DIRS if n is G_GROUPS else pl.ds(G_SIZE * n, G_SIZE)
        return halo(g_all.at[fields, edges[side]], g_halo.at[side, fields], g_send, g_recv, n, side)

    def begin(n, _):
        for side in range(2):
            f_copy(n, side).start()
        return 0

    lax.fori_loop(0, F_GROUPS, begin, 0)
    begin(F_GROUPS, 0)

    for load in loads:
        load.wait()
    row = lax.broadcasted_iota(jnp.int32, (BLOCKS * 8, 128), 0)
    for step in range(2):
        phase = jnp.full((8, 128), start_ref[0], jnp.int32) + (1 - step)
        turn = lax.rem(phase, jnp.full((8, 128), 64, jnp.int32)).astype(F32)
        half = 0.5 * (1.0 + 0.5 * jnp.sin(2.0 * math.pi * turn / 64.0))
        half = jnp.broadcast_to(half[0:1], (BLOCKS * 8, 128))

        def prepare(x, _, step=step, half=half):
            spot = pl.ds(BLOCKS * x, BLOCKS)
            d = layer(dif, (), x)
            values = [1.0 - 6.0 * d]
            for axis in range(3):
                drift = half * layer(vel, (axis,), x)
                values += [d + drift, d - drift]
            values[3] = jnp.where(row == BLOCKS * 8 - 1, 0.0, values[3])
            values[4] = jnp.where(row == 0, 0.0, values[4])
            for n in range(7):
                coef[step, n, spot] = values[n].reshape(BLOCKS, 8, 128)
            return 0

        lax.fori_loop(0, LAYERS, prepare, 0)

    def advance(step, source, landing, target, n, layers):
        for x in layers:
            here = layer(source, (n,), x)
            ahead = layer(source, (n,), x + 1) if x < LAYERS - 1 else landing[1, n].reshape(BLOCKS * 8, 128)
            behind = layer(source, (n,), x - 1) if x > 0 else landing[0, n].reshape(BLOCKS * 8, 128)
            out = stencil(here, ahead, behind, coef, step, x)
            if n is DIRS:
                out = out + layer(src, (), x)
            target[n, pl.ds(BLOCKS * x, BLOCKS)] = out.reshape(BLOCKS, 8, 128)

    def first(group, fields):
        for n in fields:
            advance(0, f_all, f_halo, g_all, n, (0, 3))
        for side in range(2):
            g_copy(group, side).start()
        for n in fields:
            advance(0, f_all, f_halo, g_all, n, (1, 2))

    def first_pair(p, _):
        first(p, [G_SIZE * p + n for n in range(G_SIZE)])
        return 0

    def first_group(q, _):
        for side in range(2):
            f_copy(q, side).wait_recv()
        ratio = F_SIZE // G_SIZE
        return lax.fori_loop(ratio * q, ratio * (q + 1), first_pair, 0)

    lax.fori_loop(0, F_GROUPS, first_group, 0)
    for side in range(2):
        f_copy(F_GROUPS, side).wait_recv()
    first(G_GROUPS, [DIRS])

    lane = lax.broadcasted_iota(jnp.int32, (DIRS, 128), 1)

    def products(n, low, total):
        def at(p, total):
            return total + w_all[0:DIRS, p] * w_all[n, p][None]

        return lax.fori_loop(low, low + BLOCKS, at, total, unroll=4)

    def second(group, fields):
        totals = []
        for n in fields:
            advance(1, g_all, g_halo, w_all, n, (1, 2))
            total = jnp.zeros((DIRS, 8, 128), F32)
            if n is DIRS:
                for x in (1, 2):
                    total = products(n, BLOCKS * x, total)
            totals.append(total)
        for side in range(2):
            g_copy(group, side).wait_recv()
        for n in fields:
            advance(1, g_all, g_halo, w_all, n, (0, 3))
        sums = []
        for n, total in zip(fields, totals):
            for x in (0, 3) if n is DIRS else range(LAYERS):
                total = products(n, BLOCKS * x, total)
            sums.append(jnp.sum(jnp.sum(total, axis=1), axis=1, keepdims=True))
        return sums

    def gram_pair(p, _):
        fields = [G_SIZE * p + n for n in range(G_SIZE)]
        for n, column in zip(fields, second(p, fields)):
            gram[...] = jnp.where(lane == n, column, gram[...])
        return 0

    lax.fori_loop(0, G_GROUPS, gram_pair, 0)

    def exchange(cur, got, send, recv, k):
        base = sum(len(stage) for stage in stages[:k])
        return [
            pltpu.make_async_remote_copy(
                cur.at[k], got.at[base + n], send.at[base + n], recv.at[base + n],
                device_id={"space": peer}, device_id_type=MESH,
            )
            for n, peer in enumerate(stages[k])
        ]

    gram_parts = functools.partial(exchange, gram_cur, gram_got, gram_send, gram_recv)
    along_parts = functools.partial(exchange, along_cur, along_got, along_send, along_recv)

    def collect(parts, cur, got, k):
        base = sum(len(stage) for stage in stages[:k])
        for copy in parts(k):
            copy.wait_recv()
        total = cur[k]
        for n in range(len(stages[k])):
            total = total + got[base + n]
        cur[k + 1] = total

    sublane = lax.broadcasted_iota(jnp.int32, (DIRS, 128), 0)
    diagonal = lane == sublane
    group_of = lane // DIRS == sublane % 8
    packed = pltpu.roll(gram[...], 0, 1, stride=DIRS, stride_axis=0)
    for h in range(2):
        gram_cur[0, h:h + 1, :] = jnp.sum(packed[8 * h:8 * h + 8], axis=0, keepdims=True)
    for copy in gram_parts(0):
        copy.start()
    along_cur[0] = jnp.sum(jnp.where(diagonal, second(G_GROUPS, [DIRS])[0], 0.0), axis=0, keepdims=True)
    for copy in along_parts(0):
        copy.start()
    count = len(stages)
    for k in range(count):
        collect(gram_parts, gram_cur, gram_got, k)
        if k + 1 < count:
            for copy in gram_parts(k + 1):
                copy.start()
            collect(along_parts, along_cur, along_got, k)
            for copy in along_parts(k + 1):
                copy.start()

    packed = jnp.concatenate(
        [jnp.broadcast_to(gram_cur[count, h:h + 1, :], (8, 128)) for h in range(2)], axis=0
    )
    whole = jnp.where(group_of, packed * (1.0 / cells), 0.0)
    for bit in (1, 2, 4):
        moved = pltpu.roll(whole, 128 - DIRS * bit, 1)
        whole = jnp.where(lax.rem(sublane // bit, 2) == 1, moved, whole)
    for j in range(DIRS):
        columns[j] = jnp.broadcast_to(whole[:, j:j + 1], (DIRS, 128))
    lane8 = lax.broadcasted_iota(jnp.int32, (8, 128), 1)
    cols = [jnp.broadcast_to(columns[k:DIRS, k:k + 1, :], (DIRS - k, 8, 128)) for k in range(DIRS)]
    rows = [
        jnp.broadcast_to(whole[i:i + 1], (8, 128)) + jnp.where(lane8 == 32 + i, 1.0, 0.0) for i in range(DIRS)
    ]
    for k in range(DIRS):
        scale = lax.rsqrt(cols[k][0])
        lower = cols[k] * scale[None]
        done = rows[k] * scale
        inverse_rows[k:k + 1, :] = done[0:1]
        for j in range(k + 1, DIRS):
            cols[j] = cols[j] - lower[j - k:] * lower[j - k][None]
            rows[j] = rows[j] - lower[j - k] * done
    solved = inverse_rows[...]
    for k in range(DIRS):
        spread[k] = jnp.broadcast_to(solved[:, 32 + k:33 + k], (DIRS, 128))

    collect(along_parts, along_cur, along_got, count - 1)
    along = along_cur[count] * (1.0 / cells)
    shifted = pltpu.roll(solved, 96, 1)
    found = jnp.sum(shifted * along, axis=1, keepdims=True)
    weight_row = jnp.sum(shifted * found, axis=0, keepdims=True)
    for k in range(DIRS):
        weights[k] = jnp.broadcast_to(weight_row[:, k:k + 1], (8, 128))

    def piece(t):
        for x in range(LAYERS):
            for h in range(2):
                p = BLOCKS * x + 2 * t + h
                value = w_all[DIRS, p]
                for k in range(DIRS):
                    value = value - weights[k] * w_all[k, p]
                shadow_ref[p] = value
                terms[t, 2 * x + h] = value + g_all[DIRS, p]

    term_copies = [
        pltpu.make_async_remote_copy(
            terms.at[lax.rem(seg + d, segs)], arrived.at[d - 1], term_send.at[d - 1], term_recv.at[d - 1],
            device_id={"seg": lax.rem(seg + d, segs)}, device_id_type=MESH,
        )
        for d in range(1, segs)
    ]
    for d in (2, 3, 1):
        piece(lax.rem(seg + d, segs))
        term_copies[d - 1].start()
    piece(seg)

    upper_ref[...] = jnp.where(lane >= sublane, solved, 0.0)[:, 0:DIRS]
    coef_ref[...] = jnp.sum(jnp.where(diagonal, found, 0.0), axis=0, keepdims=True)[:, 0:DIRS]

    for k in range(DIRS):
        for i in range(k, DIRS):
            inverse[i, k] = jnp.broadcast_to(spread[k, i:i + 1, :], (8, 128))

    def rows_at(q, _):
        spot = pl.ds(2 * q, 2)
        values = [w_all[k, spot] for k in range(DIRS)]
        for i in range(DIRS):
            total = inverse[i, 0][None] * values[0]
            for k in range(1, i + 1):
                total = total + inverse[i, k][None] * values[k]
            basis_ref[i, spot] = total
        return 0

    lax.fori_loop(0, POS // 2, rows_at, 0)

    def sent_f(n, _):
        for side in range(2):
            f_copy(n, side).wait_send()
        return 0

    def sent_g(n, _):
        for side in range(2):
            g_copy(n, side).wait_send()
        return 0

    lax.fori_loop(0, F_GROUPS, sent_f, 0)
    sent_f(F_GROUPS, 0)
    lax.fori_loop(0, G_GROUPS, sent_g, 0)
    sent_g(G_GROUPS, 0)
    for k in range(count):
        for copy in gram_parts(k) + along_parts(k):
            copy.wait_send()
    for copy in term_copies:
        copy.wait_recv()
    grad_ref[...] = terms[seg] + arrived[0] + arrived[1] + arrived[2]
    for copy in term_copies:
        copy.wait_send()


def in_hbm(array):
    return pltpu.with_memory_space_constraint(array, pltpu.HBM)


def in_vmem(array):
    return pltpu.with_memory_space_constraint(array, pltpu.VMEM)


def store_kernel(*refs):
    held, out, sems = refs[:5], refs[5:10], refs[10]
    part = DIRS // STORES
    copies = [
        pltpu.make_async_copy(held[0].at[pl.ds(part * n, part)], out[0].at[pl.ds(part * n, part)], sems.at[n])
        for n in range(STORES)
    ]
    copies += [pltpu.make_async_copy(held[n], out[n], sems.at[STORES + n - 1]) for n in range(1, 5)]
    for copy in copies:
        copy.start()
    for copy in copies:
        copy.wait()


def body(directions, adjoint, velocity, diffusivity, objective_source, segment_start):
    size, segs = lax.axis_size("space"), lax.axis_size("seg")
    tile = (POS, 8, 128)
    cells = POS * 8 * 128 * size
    height, width, depth = place_of(size)
    groups = [n for n in (height * width, depth) if n > 1]
    peers, count = sum(groups) - len(groups), len(groups)
    hbm, vmem = pl.BlockSpec(memory_space=pltpu.HBM), pl.BlockSpec(memory_space=pltpu.VMEM)
    dma = pltpu.SemaphoreType.DMA
    shapes = (
        jax.ShapeDtypeStruct((DIRS, *tile), F32),
        jax.ShapeDtypeStruct((DIRS, DIRS), F32),
        jax.ShapeDtypeStruct((1, DIRS), F32),
        jax.ShapeDtypeStruct(tile, F32),
        jax.ShapeDtypeStruct((2 * LAYERS, 8, 128), F32),
    )
    outs = pl.pallas_call(
        functools.partial(kernel, size, segs, cells),
        out_shape=tuple(pltpu.VMEM(s.shape, F32) for s in shapes),
        in_specs=[pl.BlockSpec(memory_space=pltpu.SMEM)] + [hbm] * 5,
        out_specs=(vmem,) * 5,
        scratch_shapes=[
            pltpu.VMEM((FIELDS, *tile), F32),
            pltpu.VMEM((FIELDS, *tile), F32),
            pltpu.VMEM((FIELDS, *tile), F32),
            pltpu.VMEM((2, FIELDS, BLOCKS, 8, 128), F32),
            pltpu.VMEM((2, FIELDS, BLOCKS, 8, 128), F32),
            pltpu.VMEM((2, 7, *tile), F32),
            pltpu.VMEM((3, *tile), F32),
            pltpu.VMEM(tile, F32),
            pltpu.VMEM(tile, F32),
            pltpu.VMEM((DIRS, 128), F32),
            pltpu.VMEM((count + 1, 2, 128), F32),
            pltpu.VMEM((peers, 2, 128), F32),
            pltpu.VMEM((count + 1, 1, 128), F32),
            pltpu.VMEM((peers, 1, 128), F32),
            pltpu.VMEM((DIRS, DIRS, 128), F32),
            pltpu.VMEM((DIRS, 128), F32),
            pltpu.VMEM((DIRS, DIRS, 128), F32),
            pltpu.VMEM((DIRS, DIRS, 8, 128), F32),
            pltpu.VMEM((DIRS, 8, 128), F32),
            pltpu.VMEM((4, 2 * LAYERS, 8, 128), F32),
            pltpu.VMEM((3, 2 * LAYERS, 8, 128), F32),
            dma((5,)),
            dma((2, F_GROUPS + 1)), dma((2, F_GROUPS + 1)), dma((2, G_GROUPS + 1)), dma((2, G_GROUPS + 1)),
            dma((peers,)), dma((peers,)), dma((peers,)), dma((peers,)),
            dma((3,)), dma((3,)),
        ],
        compiler_params=pltpu.CompilerParams(
            collective_id=0, has_side_effects=True, vmem_limit_bytes=40 * 1024 * 1024
        ),
        cost_estimate=pl.CostEstimate(flops=120_000_000, bytes_accessed=5_200_000, transcendentals=64),
        name="shadowing",
    )(
        segment_start,
        in_hbm(directions.reshape(DIRS, *tile)),
        in_hbm(adjoint.reshape(tile)),
        in_hbm(velocity.reshape(3, *tile)),
        in_hbm(diffusivity.reshape(tile)),
        in_hbm(objective_source.reshape(tile)),
    )
    basis_rows, upper, coefficients, shadow, gradient = pl.pallas_call(
        store_kernel,
        out_shape=shapes,
        in_specs=[pl.BlockSpec(memory_space=pl.ANY)] * 5,
        out_specs=(hbm,) * 5,
        scratch_shapes=[dma((STORES + 4,))],
        compiler_params=pltpu.CompilerParams(vmem_limit_bytes=1024 * 1024),
        name="store",
    )(*map(in_vmem, outs))
    return (
        basis_rows.reshape(directions.shape),
        upper[None],
        coefficients,
        shadow.reshape(adjoint.shape),
        gradient.reshape(LAYERS, 16, 128),
    )


def solution(mesh):
    return jax.shard_map(
        body,
        mesh=mesh,
        in_specs=(
            P("seg", None, "space", None, None),
            P("seg", "space", None, None),
            P("seg", None, "space", None, None),
            P("seg", "space", None, None),
            P("seg", "space", None, None),
            P("seg"),
        ),
        out_specs=(
            P("seg", None, "space", None, None),
            P("seg", None, None),
            P("seg", None),
            P("seg", "space", None, None),
            P("space", "seg", None),
        ),
        check_vma=False,
    )
```

```python
import functools
import math

import jax
import jax.numpy as jnp
from jax import lax
from jax.experimental import pallas as pl
from jax.experimental.pallas import tpu as pltpu
from jax.sharding import PartitionSpec as P

MESH = pl.DeviceIdType.MESH
DIRS = 16
FIELDS = 17
F_SIZE, G_SIZE = 4, 2
F_GROUPS, G_GROUPS = DIRS // F_SIZE, DIRS // G_SIZE
LAYERS = 4
STORES = 1
BLOCKS = 8
POS = LAYERS * BLOCKS
F32 = jnp.float32


def place_of(size):
    depth = min(4, size)
    width = min(4, size // depth)
    height = size // (depth * width)
    return height, width, depth


def peers_of(me, size):
    height, width, depth = place_of(size)
    z = lax.rem(me, depth)
    x = lax.rem(lax.div(me, depth), width)
    y = lax.div(me, depth * width)
    stages = [
        [
            ((y + 1 - 2 * lax.rem(y, 2) if a else y) * width + lax.rem(x + b, width)) * depth + z
            for a in range(2) for b in range(width) if a or b
        ],
        [
            ((height - 1 - y if a else y) * width + x) * depth + lax.rem(z + d, depth)
            for a in range(2) for d in range(depth) if a or d
        ],
    ]
    return [stage for stage in stages if stage]


def layer(ref, lead, x):
    return ref[(*lead, pl.ds(BLOCKS * x, BLOCKS))].reshape(BLOCKS * 8, 128)


def stencil(here, ahead, behind, coef, step, x):
    c = [layer(coef, (step, n), x) for n in range(7)]
    out = c[0] * here + c[1] * ahead + c[2] * behind
    out = out + c[3] * pltpu.roll(here, BLOCKS * 8 - 1, 0) + c[4] * pltpu.roll(here, 1, 0)
    return out + c[5] * pltpu.roll(here, 127, 1) + c[6] * pltpu.roll(here, 1, 1)


def kernel(
    size, segs, cells,
    start_ref, dirs_ref, adj_ref, vel_ref, dif_ref, src_ref,
    basis_ref, upper_ref, coef_ref, shadow_ref, grad_ref,
    f_all, g_all, w_all, f_halo, g_halo, coef, vel, dif, src,
    gram, gram_cur, gram_got, along_cur, along_got, columns, inverse_rows, spread, inverse, weights, terms, arrived,
    load_sem, f_send, f_recv, g_send, g_recv,
    gram_send, gram_recv, along_send, along_recv, term_send, term_recv,
):
    seg = lax.axis_index("seg")
    me = lax.axis_index("space")
    right, left = lax.rem(me + 1, size), lax.rem(me + size - 1, size)
    stages = peers_of(me, size)

    barrier = pltpu.get_barrier_semaphore()
    greeted = [{"space": left}, {"space": right}]
    greeted += [{"space": peer} for stage in stages for peer in stage]
    partners = [lax.rem(seg + 2, segs), segs - 1 - seg, seg + 1 - 2 * lax.rem(seg, 2)]
    greeted += [{"seg": partner} for partner in partners]
    for device in greeted:
        pl.semaphore_signal(barrier, inc=1, device_id=device, device_id_type=MESH)

    loads = [
        pltpu.make_async_copy(dirs_ref, f_all.at[pl.ds(0, DIRS)], load_sem.at[0]),
        pltpu.make_async_copy(adj_ref, f_all.at[DIRS], load_sem.at[1]),
        pltpu.make_async_copy(vel_ref, vel, load_sem.at[2]),
        pltpu.make_async_copy(dif_ref, dif, load_sem.at[3]),
        pltpu.make_async_copy(src_ref, src, load_sem.at[4]),
    ]
    for load in loads:
        load.start()

    def clear(n, _):
        w_all[n] = jnp.zeros((POS, 8, 128), F32)
        return 0

    lax.fori_loop(0, FIELDS, clear, 0)
    gram[...] = jnp.zeros_like(gram)
    pl.semaphore_wait(barrier, len(greeted))

    def halo(source, landing, send, recv, n, side):
        return pltpu.make_async_remote_copy(
            source,
            landing,
            send.at[side, n],
            recv.at[side, n],
            device_id={"space": right if side == 0 else left},
            device_id_type=MESH,
        )

    edges = (pl.ds(BLOCKS * (LAYERS - 1), BLOCKS), pl.ds(0, BLOCKS))

    def f_copy(n, side):
        if n is F_GROUPS:
            return halo(adj_ref.at[edges[side]], f_halo.at[side, DIRS], f_send, f_recv, n, side)
        fields = pl.ds(F_SIZE * n, F_SIZE)
        return halo(dirs_ref.at[fields, edges[side]], f_halo.at[side, fields], f_send, f_recv, n, side)

    def g_copy(n, side):
        fields = DIRS if n is G_GROUPS else pl.ds(G_SIZE * n, G_SIZE)
        return halo(g_all.at[fields, edges[side]], g_halo.at[side, fields], g_send, g_recv, n, side)

    def begin(n, _):
        for side in range(2):
            f_copy(n, side).start()
        return 0

    lax.fori_loop(0, F_GROUPS, begin, 0)
    begin(F_GROUPS, 0)

    for load in loads:
        load.wait()
    row = lax.broadcasted_iota(jnp.int32, (BLOCKS * 8, 128), 0)
    for step in range(2):
        phase = jnp.full((8, 128), start_ref[0], jnp.int32) + (1 - step)
        turn = lax.rem(phase, jnp.full((8, 128), 64, jnp.int32)).astype(F32)
        half = 0.5 * (1.0 + 0.5 * jnp.sin(2.0 * math.pi * turn / 64.0))
        half = jnp.broadcast_to(half[0:1], (BLOCKS * 8, 128))

        def prepare(x, _, step=step, half=half):
            spot = pl.ds(BLOCKS * x, BLOCKS)
            d = layer(dif, (), x)
            values = [1.0 - 6.0 * d]
            for axis in range(3):
                drift = half * layer(vel, (axis,), x)
                values += [d + drift, d - drift]
            values[3] = jnp.where(row == BLOCKS * 8 - 1, 0.0, values[3])
            values[4] = jnp.where(row == 0, 0.0, values[4])
            for n in range(7):
                coef[step, n, spot] = values[n].reshape(BLOCKS, 8, 128)
            return 0

        lax.fori_loop(0, LAYERS, prepare, 0)

    def advance(step, source, landing, target, n, layers):
        for x in layers:
            here = layer(source, (n,), x)
            ahead = layer(source, (n,), x + 1) if x < LAYERS - 1 else landing[1, n].reshape(BLOCKS * 8, 128)
            behind = layer(source, (n,), x - 1) if x > 0 else landing[0, n].reshape(BLOCKS * 8, 128)
            out = stencil(here, ahead, behind, coef, step, x)
            target[n, pl.ds(BLOCKS * x, BLOCKS)] = out.reshape(BLOCKS, 8, 128)

        @pl.when(n == DIRS)
        def _():
            for x in layers:
                spot = pl.ds(BLOCKS * x, BLOCKS)
                target[n, spot] = target[n, spot] + src[spot]

    def each(p, work):
        def one(n, _):
            work(n)
            return 0

        lax.fori_loop(G_SIZE * p, jnp.minimum(G_SIZE * (p + 1), FIELDS), one, 0)

    def either(p, work):
        pl.when(p < G_GROUPS)(lambda: work(p))
        pl.when(p == G_GROUPS)(lambda: work(G_GROUPS))

    def both_sides(action):
        for side in range(2):
            action(side)

    ratio = F_SIZE // G_SIZE

    def first(p, _):
        @pl.when(jnp.logical_and(p < G_GROUPS, lax.rem(p, ratio) == 0))
        def _():
            both_sides(lambda side: f_copy(lax.div(p, ratio), side).wait_recv())

        @pl.when(p == G_GROUPS)
        def _():
            both_sides(lambda side: f_copy(F_GROUPS, side).wait_recv())

        each(p, lambda n: advance(0, f_all, f_halo, g_all, n, (0, 3)))
        either(p, lambda group: both_sides(lambda side: g_copy(group, side).start()))
        each(p, lambda n: advance(0, f_all, f_halo, g_all, n, (1, 2)))
        return 0

    lax.fori_loop(0, G_GROUPS + 1, first, 0)

    lane = lax.broadcasted_iota(jnp.int32, (DIRS, 128), 1)

    def exchange(cur, got, send, recv, k):
        base = sum(len(stage) for stage in stages[:k])
        return [
            pltpu.make_async_remote_copy(
                cur.at[k], got.at[base + n], send.at[base + n], recv.at[base + n],
                device_id={"space": peer}, device_id_type=MESH,
            )
            for n, peer in enumerate(stages[k])
        ]

    gram_parts = functools.partial(exchange, gram_cur, gram_got, gram_send, gram_recv)
    along_parts = functools.partial(exchange, along_cur, along_got, along_send, along_recv)

    def collect(parts, cur, got, k):
        base = sum(len(stage) for stage in stages[:k])
        for copy in parts(k):
            copy.wait_recv()
        total = cur[k]
        for n in range(len(stages[k])):
            total = total + got[base + n]
        cur[k + 1] = total

    sublane = lax.broadcasted_iota(jnp.int32, (DIRS, 128), 0)
    diagonal = lane == sublane
    group_of = lane // DIRS == sublane % 8
    def gram_row(n):
        def at(p, total):
            return total + w_all[0:DIRS, p] * w_all[n, p][None]

        total = lax.fori_loop(0, POS, at, jnp.zeros((DIRS, 8, 128), F32), unroll=4)
        column = jnp.sum(jnp.sum(total, axis=1), axis=1, keepdims=True)
        gram[...] = jnp.where(lane == n, column, gram[...])

    def second(p, _):
        @pl.when(p == G_GROUPS)
        def _():
            packed = pltpu.roll(gram[...], 0, 1, stride=DIRS, stride_axis=0)
            for h in range(2):
                gram_cur[0, h:h + 1, :] = jnp.sum(packed[8 * h:8 * h + 8], axis=0, keepdims=True)
            for copy in gram_parts(0):
                copy.start()

        each(p, lambda n: advance(1, g_all, g_halo, w_all, n, (1, 2)))
        either(p, lambda group: both_sides(lambda side: g_copy(group, side).wait_recv()))
        each(p, lambda n: advance(1, g_all, g_halo, w_all, n, (0, 3)))
        each(p, gram_row)
        return 0

    lax.fori_loop(0, G_GROUPS + 1, second, 0)
    along_column = jnp.broadcast_to(gram[:, DIRS:DIRS + 1], (DIRS, 128))
    along_cur[0] = jnp.sum(jnp.where(diagonal, along_column, 0.0), axis=0, keepdims=True)
    for copy in along_parts(0):
        copy.start()
    count = len(stages)
    for k in range(count):
        collect(gram_parts, gram_cur, gram_got, k)
        if k + 1 < count:
            for copy in gram_parts(k + 1):
                copy.start()
            collect(along_parts, along_cur, along_got, k)
            for copy in along_parts(k + 1):
                copy.start()

    packed = jnp.concatenate(
        [jnp.broadcast_to(gram_cur[count, h:h + 1, :], (8, 128)) for h in range(2)], axis=0
    )
    whole = jnp.where(group_of, packed * (1.0 / cells), 0.0)
    for bit in (1, 2, 4):
        moved = pltpu.roll(whole, 128 - DIRS * bit, 1)
        whole = jnp.where(lax.rem(sublane // bit, 2) == 1, moved, whole)
    for j in range(DIRS):
        columns[j] = jnp.broadcast_to(whole[:, j:j + 1], (DIRS, 128))
    lane8 = lax.broadcasted_iota(jnp.int32, (8, 128), 1)
    cols = [jnp.broadcast_to(columns[k:DIRS, k:k + 1, :], (DIRS - k, 8, 128)) for k in range(DIRS)]
    rows = [
        jnp.broadcast_to(whole[i:i + 1], (8, 128)) + jnp.where(lane8 == 32 + i, 1.0, 0.0) for i in range(DIRS)
    ]
    for k in range(DIRS):
        scale = lax.rsqrt(cols[k][0])
        lower = cols[k] * scale[None]
        done = rows[k] * scale
        inverse_rows[k:k + 1, :] = done[0:1]
        for j in range(k + 1, DIRS):
            cols[j] = cols[j] - lower[j - k:] * lower[j - k][None]
            rows[j] = rows[j] - lower[j - k] * done
    solved = inverse_rows[...]
    for k in range(DIRS):
        spread[k] = jnp.broadcast_to(solved[:, 32 + k:33 + k], (DIRS, 128))

    collect(along_parts, along_cur, along_got, count - 1)
    along = along_cur[count] * (1.0 / cells)
    shifted = pltpu.roll(solved, 96, 1)
    found = jnp.sum(shifted * along, axis=1, keepdims=True)
    weight_row = jnp.sum(shifted * found, axis=0, keepdims=True)
    for k in range(DIRS):
        weights[k] = jnp.broadcast_to(weight_row[:, k:k + 1], (8, 128))

    def piece(t):
        for x in range(LAYERS):
            for h in range(2):
                p = BLOCKS * x + 2 * t + h
                value = w_all[DIRS, p]
                for k in range(DIRS):
                    value = value - weights[k] * w_all[k, p]
                shadow_ref[p] = value
                terms[t, 2 * x + h] = value + g_all[DIRS, p]

    term_copies = [
        pltpu.make_async_remote_copy(
            terms.at[partner], arrived.at[n], term_send.at[n], term_recv.at[n],
            device_id={"seg": partner}, device_id_type=MESH,
        )
        for n, partner in enumerate(partners)
    ]
    for partner, copy in zip(partners, term_copies):
        piece(partner)
        copy.start()
    piece(seg)

    upper_ref[...] = jnp.where(lane >= sublane, solved, 0.0)[:, 0:DIRS]
    coef_ref[...] = jnp.sum(jnp.where(diagonal, found, 0.0), axis=0, keepdims=True)[:, 0:DIRS]

    for k in range(DIRS):
        for i in range(k, DIRS):
            inverse[i, k] = jnp.broadcast_to(spread[k, i:i + 1, :], (8, 128))

    def rows_at(q, _):
        spot = pl.ds(2 * q, 2)
        values = [w_all[k, spot] for k in range(DIRS)]
        for i in range(DIRS):
            total = inverse[i, 0][None] * values[0]
            for k in range(1, i + 1):
                total = total + inverse[i, k][None] * values[k]
            basis_ref[i, spot] = total
        return 0

    lax.fori_loop(0, POS // 2, rows_at, 0)

    def sent_f(n, _):
        for side in range(2):
            f_copy(n, side).wait_send()
        return 0

    def sent_g(n, _):
        for side in range(2):
            g_copy(n, side).wait_send()
        return 0

    lax.fori_loop(0, F_GROUPS, sent_f, 0)
    sent_f(F_GROUPS, 0)
    lax.fori_loop(0, G_GROUPS, sent_g, 0)
    sent_g(G_GROUPS, 0)
    for k in range(count):
        for copy in gram_parts(k) + along_parts(k):
            copy.wait_send()
    for copy in term_copies:
        copy.wait_recv()
    grad_ref[...] = terms[seg] + arrived[0] + arrived[1] + arrived[2]
    for copy in term_copies:
        copy.wait_send()


def in_hbm(array):
    return pltpu.with_memory_space_constraint(array, pltpu.HBM)


def in_vmem(array):
    return pltpu.with_memory_space_constraint(array, pltpu.VMEM)


def store_kernel(*refs):
    held, out, sems = refs[:5], refs[5:10], refs[10]
    part = DIRS // STORES
    copies = [
        pltpu.make_async_copy(held[0].at[pl.ds(part * n, part)], out[0].at[pl.ds(part * n, part)], sems.at[n])
        for n in range(STORES)
    ]
    copies += [pltpu.make_async_copy(held[n], out[n], sems.at[STORES + n - 1]) for n in range(1, 5)]
    for copy in copies:
        copy.start()
    for copy in copies:
        copy.wait()


def body(directions, adjoint, velocity, diffusivity, objective_source, segment_start):
    size, segs = lax.axis_size("space"), lax.axis_size("seg")
    tile = (POS, 8, 128)
    cells = POS * 8 * 128 * size
    height, width, depth = place_of(size)
    groups = [8, 8]
    peers, count = sum(groups) - len(groups), len(groups)
    hbm, vmem = pl.BlockSpec(memory_space=pltpu.HBM), pl.BlockSpec(memory_space=pltpu.VMEM)
    dma = pltpu.SemaphoreType.DMA
    shapes = (
        jax.ShapeDtypeStruct((DIRS, *tile), F32),
        jax.ShapeDtypeStruct((DIRS, DIRS), F32),
        jax.ShapeDtypeStruct((1, DIRS), F32),
        jax.ShapeDtypeStruct(tile, F32),
        jax.ShapeDtypeStruct((2 * LAYERS, 8, 128), F32),
    )
    outs = pl.pallas_call(
        functools.partial(kernel, size, segs, cells),
        out_shape=tuple(pltpu.VMEM(s.shape, F32) for s in shapes),
        in_specs=[pl.BlockSpec(memory_space=pltpu.SMEM)] + [hbm] * 5,
        out_specs=(vmem,) * 5,
        scratch_shapes=[
            pltpu.VMEM((FIELDS, *tile), F32),
            pltpu.VMEM((FIELDS, *tile), F32),
            pltpu.VMEM((FIELDS, *tile), F32),
            pltpu.VMEM((2, FIELDS, BLOCKS, 8, 128), F32),
            pltpu.VMEM((2, FIELDS, BLOCKS, 8, 128), F32),
            pltpu.VMEM((2, 7, *tile), F32),
            pltpu.VMEM((3, *tile), F32),
            pltpu.VMEM(tile, F32),
            pltpu.VMEM(tile, F32),
            pltpu.VMEM((DIRS, 128), F32),
            pltpu.VMEM((count + 1, 2, 128), F32),
            pltpu.VMEM((peers, 2, 128), F32),
            pltpu.VMEM((count + 1, 1, 128), F32),
            pltpu.VMEM((peers, 1, 128), F32),
            pltpu.VMEM((DIRS, DIRS, 128), F32),
            pltpu.VMEM((DIRS, 128), F32),
            pltpu.VMEM((DIRS, DIRS, 128), F32),
            pltpu.VMEM((DIRS, DIRS, 8, 128), F32),
            pltpu.VMEM((DIRS, 8, 128), F32),
            pltpu.VMEM((4, 2 * LAYERS, 8, 128), F32),
            pltpu.VMEM((3, 2 * LAYERS, 8, 128), F32),
            dma((5,)),
            dma((2, F_GROUPS + 1)), dma((2, F_GROUPS + 1)), dma((2, G_GROUPS + 1)), dma((2, G_GROUPS + 1)),
            dma((peers,)), dma((peers,)), dma((peers,)), dma((peers,)),
            dma((3,)), dma((3,)),
        ],
        compiler_params=pltpu.CompilerParams(
            collective_id=0, has_side_effects=True, vmem_limit_bytes=40 * 1024 * 1024
        ),
        cost_estimate=pl.CostEstimate(flops=120_000_000, bytes_accessed=5_200_000, transcendentals=64),
        name="shadowing",
    )(
        segment_start,
        in_hbm(directions.reshape(DIRS, *tile)),
        in_hbm(adjoint.reshape(tile)),
        in_hbm(velocity.reshape(3, *tile)),
        in_hbm(diffusivity.reshape(tile)),
        in_hbm(objective_source.reshape(tile)),
    )
    basis_rows, upper, coefficients, shadow, gradient = pl.pallas_call(
        store_kernel,
        out_shape=shapes,
        in_specs=[pl.BlockSpec(memory_space=pl.ANY)] * 5,
        out_specs=(hbm,) * 5,
        scratch_shapes=[dma((STORES + 4,))],
        compiler_params=pltpu.CompilerParams(vmem_limit_bytes=1024 * 1024),
        name="store",
    )(*map(in_vmem, outs))
    return (
        basis_rows.reshape(directions.shape),
        upper[None],
        coefficients,
        shadow.reshape(adjoint.shape),
        gradient.reshape(LAYERS, 16, 128),
    )


def solution(mesh):
    return jax.shard_map(
        body,
        mesh=mesh,
        in_specs=(
            P("seg", None, "space", None, None),
            P("seg", "space", None, None),
            P("seg", None, "space", None, None),
            P("seg", "space", None, None),
            P("seg", "space", None, None),
            P("seg"),
        ),
        out_specs=(
            P("seg", None, "space", None, None),
            P("seg", None, None),
            P("seg", None),
            P("seg", "space", None, None),
            P("space", "seg", None),
        ),
        check_vma=False,
    )
```

```python
import functools
import math

import jax
import jax.numpy as jnp
from jax import lax
from jax.experimental import pallas as pl
from jax.experimental.pallas import tpu as pltpu
from jax.sharding import PartitionSpec as P

MESH = pl.DeviceIdType.MESH
DIRS = 16
FIELDS = 17
F_SIZE, G_SIZE = 4, 2
F_GROUPS, G_GROUPS = DIRS // F_SIZE, DIRS // G_SIZE
LAYERS = 4
STORES = 1
BLOCKS = 8
POS = LAYERS * BLOCKS
F32 = jnp.float32


def place_of(size):
    depth = min(4, size)
    width = min(4, size // depth)
    height = size // (depth * width)
    return height, width, depth


def peers_of(me, size):
    height, width, depth = place_of(size)
    z = lax.rem(me, depth)
    x = lax.rem(lax.div(me, depth), width)
    y = lax.div(me, depth * width)
    stages = [
        [
            ((y + 1 - 2 * lax.rem(y, 2) if a else y) * width + lax.rem(x + b, width)) * depth + z
            for a in range(2) for b in range(width) if a or b
        ],
        [
            ((height - 1 - y if a else y) * width + x) * depth + lax.rem(z + d, depth)
            for a in range(2) for d in range(depth) if a or d
        ],
    ]
    return [stage for stage in stages if stage]


def layer(ref, lead, x):
    return ref[(*lead, pl.ds(BLOCKS * x, BLOCKS))].reshape(BLOCKS * 8, 128)


def stencil(here, ahead, behind, coef, step, x):
    c = [layer(coef, (step, n), x) for n in range(7)]
    out = c[0] * here + c[1] * ahead + c[2] * behind
    out = out + c[3] * pltpu.roll(here, BLOCKS * 8 - 1, 0) + c[4] * pltpu.roll(here, 1, 0)
    return out + c[5] * pltpu.roll(here, 127, 1) + c[6] * pltpu.roll(here, 1, 1)


def kernel(
    size, segs, cells,
    start_ref, dirs_ref, adj_ref, vel_ref, dif_ref, src_ref,
    basis_ref, upper_ref, coef_ref, shadow_ref, grad_ref,
    f_all, g_all, w_all, f_halo, g_halo, coef, vel, dif, src,
    gram, gram_cur, gram_got, along_cur, along_got, columns, inverse_rows, spread, inverse, weights, terms, arrived,
    load_sem, f_send, f_recv, g_send, g_recv,
    gram_send, gram_recv, along_send, along_recv, term_send, term_recv,
):
    seg = lax.axis_index("seg")
    me = lax.axis_index("space")
    right, left = lax.rem(me + 1, size), lax.rem(me + size - 1, size)
    stages = peers_of(me, size)

    barrier = pltpu.get_barrier_semaphore()
    greeted = [{"space": left}, {"space": right}]
    greeted += [{"space": peer} for stage in stages for peer in stage]
    partners = [lax.rem(seg + 2, segs), segs - 1 - seg, seg + 1 - 2 * lax.rem(seg, 2)]
    greeted += [{"seg": partner} for partner in partners]
    for device in greeted:
        pl.semaphore_signal(barrier, inc=1, device_id=device, device_id_type=MESH)

    loads = [
        pltpu.make_async_copy(dirs_ref, f_all.at[pl.ds(0, DIRS)], load_sem.at[0]),
        pltpu.make_async_copy(adj_ref, f_all.at[DIRS], load_sem.at[1]),
        pltpu.make_async_copy(vel_ref, vel, load_sem.at[2]),
        pltpu.make_async_copy(dif_ref, dif, load_sem.at[3]),
        pltpu.make_async_copy(src_ref, src, load_sem.at[4]),
    ]
    for load in loads:
        load.start()

    def clear(n, _):
        w_all[n] = jnp.zeros((POS, 8, 128), F32)
        return 0

    lax.fori_loop(0, FIELDS, clear, 0)
    gram[...] = jnp.zeros_like(gram)
    for load in loads:
        load.wait()
    pl.semaphore_wait(barrier, len(greeted))

    def halo(source, landing, send, recv, n, side):
        return pltpu.make_async_remote_copy(
            source,
            landing,
            send.at[side, n],
            recv.at[side, n],
            device_id={"space": right if side == 0 else left},
            device_id_type=MESH,
        )

    edges = (pl.ds(BLOCKS * (LAYERS - 1), BLOCKS), pl.ds(0, BLOCKS))

    def f_copy(n, side):
        if n is F_GROUPS:
            return halo(f_all.at[DIRS, edges[side]], f_halo.at[side, DIRS], f_send, f_recv, n, side)
        fields = pl.ds(F_SIZE * n, F_SIZE)
        return halo(f_all.at[fields, edges[side]], f_halo.at[side, fields], f_send, f_recv, n, side)

    def g_copy(n, side):
        fields = DIRS if n is G_GROUPS else pl.ds(G_SIZE * n, G_SIZE)
        return halo(g_all.at[fields, edges[side]], g_halo.at[side, fields], g_send, g_recv, n, side)

    def begin(n, _):
        for side in range(2):
            f_copy(n, side).start()
        return 0

    lax.fori_loop(0, F_GROUPS, begin, 0)
    begin(F_GROUPS, 0)

    row = lax.broadcasted_iota(jnp.int32, (BLOCKS * 8, 128), 0)
    for step in range(2):
        phase = jnp.full((8, 128), start_ref[0], jnp.int32) + (1 - step)
        turn = lax.rem(phase, jnp.full((8, 128), 64, jnp.int32)).astype(F32)
        half = 0.5 * (1.0 + 0.5 * jnp.sin(2.0 * math.pi * turn / 64.0))
        half = jnp.broadcast_to(half[0:1], (BLOCKS * 8, 128))

        def prepare(x, _, step=step, half=half):
            spot = pl.ds(BLOCKS * x, BLOCKS)
            d = layer(dif, (), x)
            values = [1.0 - 6.0 * d]
            for axis in range(3):
                drift = half * layer(vel, (axis,), x)
                values += [d + drift, d - drift]
            values[3] = jnp.where(row == BLOCKS * 8 - 1, 0.0, values[3])
            values[4] = jnp.where(row == 0, 0.0, values[4])
            for n in range(7):
                coef[step, n, spot] = values[n].reshape(BLOCKS, 8, 128)
            return 0

        lax.fori_loop(0, LAYERS, prepare, 0)

    def advance(step, source, landing, target, n, layers):
        for x in layers:
            here = layer(source, (n,), x)
            ahead = layer(source, (n,), x + 1) if x < LAYERS - 1 else landing[1, n].reshape(BLOCKS * 8, 128)
            behind = layer(source, (n,), x - 1) if x > 0 else landing[0, n].reshape(BLOCKS * 8, 128)
            out = stencil(here, ahead, behind, coef, step, x)
            target[n, pl.ds(BLOCKS * x, BLOCKS)] = out.reshape(BLOCKS, 8, 128)

        @pl.when(n == DIRS)
        def _():
            for x in layers:
                spot = pl.ds(BLOCKS * x, BLOCKS)
                target[n, spot] = target[n, spot] + src[spot]

    def each(p, work):
        def one(n, _):
            work(n)
            return 0

        lax.fori_loop(G_SIZE * p, jnp.minimum(G_SIZE * (p + 1), FIELDS), one, 0)

    def either(p, work):
        pl.when(p < G_GROUPS)(lambda: work(p))
        pl.when(p == G_GROUPS)(lambda: work(G_GROUPS))

    def both_sides(action):
        for side in range(2):
            action(side)

    ratio = F_SIZE // G_SIZE

    def first(p, _):
        @pl.when(jnp.logical_and(p < G_GROUPS, lax.rem(p, ratio) == 0))
        def _():
            both_sides(lambda side: f_copy(lax.div(p, ratio), side).wait_recv())

        @pl.when(p == G_GROUPS)
        def _():
            both_sides(lambda side: f_copy(F_GROUPS, side).wait_recv())

        each(p, lambda n: advance(0, f_all, f_halo, g_all, n, (0, 3)))
        either(p, lambda group: both_sides(lambda side: g_copy(group, side).start()))
        each(p, lambda n: advance(0, f_all, f_halo, g_all, n, (1, 2)))
        return 0

    lax.fori_loop(0, G_GROUPS + 1, first, 0)

    lane = lax.broadcasted_iota(jnp.int32, (DIRS, 128), 1)

    def exchange(cur, got, send, recv, k):
        base = sum(len(stage) for stage in stages[:k])
        return [
            pltpu.make_async_remote_copy(
                cur.at[k], got.at[base + n], send.at[base + n], recv.at[base + n],
                device_id={"space": peer}, device_id_type=MESH,
            )
            for n, peer in enumerate(stages[k])
        ]

    gram_parts = functools.partial(exchange, gram_cur, gram_got, gram_send, gram_recv)
    along_parts = functools.partial(exchange, along_cur, along_got, along_send, along_recv)

    def collect(parts, cur, got, k):
        base = sum(len(stage) for stage in stages[:k])
        for copy in parts(k):
            copy.wait_recv()
        total = cur[k]
        for n in range(len(stages[k])):
            total = total + got[base + n]
        cur[k + 1] = total

    sublane = lax.broadcasted_iota(jnp.int32, (DIRS, 128), 0)
    diagonal = lane == sublane
    group_of = lane // DIRS == sublane % 8
    def gram_row(n):
        def at(p, total):
            return total + w_all[0:DIRS, p] * w_all[n, p][None]

        total = lax.fori_loop(0, POS, at, jnp.zeros((DIRS, 8, 128), F32), unroll=4)
        column = jnp.sum(jnp.sum(total, axis=1), axis=1, keepdims=True)
        gram[...] = jnp.where(lane == n, column, gram[...])

    def second(p, _):
        @pl.when(p == G_GROUPS)
        def _():
            packed = pltpu.roll(gram[...], 0, 1, stride=DIRS, stride_axis=0)
            for h in range(2):
                gram_cur[0, h:h + 1, :] = jnp.sum(packed[8 * h:8 * h + 8], axis=0, keepdims=True)
            for copy in gram_parts(0):
                copy.start()

        each(p, lambda n: advance(1, g_all, g_halo, w_all, n, (1, 2)))
        either(p, lambda group: both_sides(lambda side: g_copy(group, side).wait_recv()))
        each(p, lambda n: advance(1, g_all, g_halo, w_all, n, (0, 3)))
        each(p, gram_row)
        return 0

    lax.fori_loop(0, G_GROUPS + 1, second, 0)
    along_column = jnp.broadcast_to(gram[:, DIRS:DIRS + 1], (DIRS, 128))
    along_cur[0] = jnp.sum(jnp.where(diagonal, along_column, 0.0), axis=0, keepdims=True)
    for copy in along_parts(0):
        copy.start()
    count = len(stages)
    for k in range(count):
        collect(gram_parts, gram_cur, gram_got, k)
        if k + 1 < count:
            for copy in gram_parts(k + 1):
                copy.start()
            collect(along_parts, along_cur, along_got, k)
            for copy in along_parts(k + 1):
                copy.start()

    packed = jnp.concatenate(
        [jnp.broadcast_to(gram_cur[count, h:h + 1, :], (8, 128)) for h in range(2)], axis=0
    )
    whole = jnp.where(group_of, packed * (1.0 / cells), 0.0)
    for bit in (1, 2, 4):
        moved = pltpu.roll(whole, 128 - DIRS * bit, 1)
        whole = jnp.where(lax.rem(sublane // bit, 2) == 1, moved, whole)
    for j in range(DIRS):
        columns[j] = jnp.broadcast_to(whole[:, j:j + 1], (DIRS, 128))
    lane8 = lax.broadcasted_iota(jnp.int32, (8, 128), 1)
    cols = [jnp.broadcast_to(columns[k:DIRS, k:k + 1, :], (DIRS - k, 8, 128)) for k in range(DIRS)]
    rows = [
        jnp.broadcast_to(whole[i:i + 1], (8, 128)) + jnp.where(lane8 == 32 + i, 1.0, 0.0) for i in range(DIRS)
    ]
    for k in range(DIRS):
        scale = lax.rsqrt(cols[k][0])
        lower = cols[k] * scale[None]
        done = rows[k] * scale
        inverse_rows[k:k + 1, :] = done[0:1]
        for j in range(k + 1, DIRS):
            cols[j] = cols[j] - lower[j - k:] * lower[j - k][None]
            rows[j] = rows[j] - lower[j - k] * done
    solved = inverse_rows[...]
    for k in range(DIRS):
        spread[k] = jnp.broadcast_to(solved[:, 32 + k:33 + k], (DIRS, 128))

    collect(along_parts, along_cur, along_got, count - 1)
    along = along_cur[count] * (1.0 / cells)
    shifted = pltpu.roll(solved, 96, 1)
    found = jnp.sum(shifted * along, axis=1, keepdims=True)
    weight_row = jnp.sum(shifted * found, axis=0, keepdims=True)
    for k in range(DIRS):
        weights[k] = jnp.broadcast_to(weight_row[:, k:k + 1], (8, 128))

    def piece(t):
        for x in range(LAYERS):
            for h in range(2):
                p = BLOCKS * x + 2 * t + h
                value = w_all[DIRS, p]
                for k in range(DIRS):
                    value = value - weights[k] * w_all[k, p]
                shadow_ref[p] = value
                terms[t, 2 * x + h] = value + g_all[DIRS, p]

    term_copies = [
        pltpu.make_async_remote_copy(
            terms.at[partner], arrived.at[n], term_send.at[n], term_recv.at[n],
            device_id={"seg": partner}, device_id_type=MESH,
        )
        for n, partner in enumerate(partners)
    ]
    for partner, copy in zip(partners, term_copies):
        piece(partner)
        copy.start()
    piece(seg)

    upper_ref[...] = jnp.where(lane >= sublane, solved, 0.0)[:, 0:DIRS]
    coef_ref[...] = jnp.sum(jnp.where(diagonal, found, 0.0), axis=0, keepdims=True)[:, 0:DIRS]

    for k in range(DIRS):
        for i in range(k, DIRS):
            inverse[i, k] = jnp.broadcast_to(spread[k, i:i + 1, :], (8, 128))

    def rows_at(q, _):
        spot = pl.ds(2 * q, 2)
        values = [w_all[k, spot] for k in range(DIRS)]
        for i in range(DIRS):
            total = inverse[i, 0][None] * values[0]
            for k in range(1, i + 1):
                total = total + inverse[i, k][None] * values[k]
            basis_ref[i, spot] = total
        return 0

    lax.fori_loop(0, POS // 2, rows_at, 0)

    def sent_f(n, _):
        for side in range(2):
            f_copy(n, side).wait_send()
        return 0

    def sent_g(n, _):
        for side in range(2):
            g_copy(n, side).wait_send()
        return 0

    lax.fori_loop(0, F_GROUPS, sent_f, 0)
    sent_f(F_GROUPS, 0)
    lax.fori_loop(0, G_GROUPS, sent_g, 0)
    sent_g(G_GROUPS, 0)
    for k in range(count):
        for copy in gram_parts(k) + along_parts(k):
            copy.wait_send()
    for copy in term_copies:
        copy.wait_recv()
    grad_ref[...] = terms[seg] + arrived[0] + arrived[1] + arrived[2]
    for copy in term_copies:
        copy.wait_send()


def in_hbm(array):
    return pltpu.with_memory_space_constraint(array, pltpu.HBM)


def in_vmem(array):
    return pltpu.with_memory_space_constraint(array, pltpu.VMEM)


def store_kernel(*refs):
    held, out, sems = refs[:5], refs[5:10], refs[10]
    part = DIRS // STORES
    copies = [
        pltpu.make_async_copy(held[0].at[pl.ds(part * n, part)], out[0].at[pl.ds(part * n, part)], sems.at[n])
        for n in range(STORES)
    ]
    copies += [pltpu.make_async_copy(held[n], out[n], sems.at[STORES + n - 1]) for n in range(1, 5)]
    for copy in copies:
        copy.start()
    for copy in copies:
        copy.wait()


def body(directions, adjoint, velocity, diffusivity, objective_source, segment_start):
    size, segs = lax.axis_size("space"), lax.axis_size("seg")
    tile = (POS, 8, 128)
    cells = POS * 8 * 128 * size
    height, width, depth = place_of(size)
    groups = [8, 8]
    peers, count = sum(groups) - len(groups), len(groups)
    hbm, vmem = pl.BlockSpec(memory_space=pltpu.HBM), pl.BlockSpec(memory_space=pltpu.VMEM)
    dma = pltpu.SemaphoreType.DMA
    shapes = (
        jax.ShapeDtypeStruct((DIRS, *tile), F32),
        jax.ShapeDtypeStruct((DIRS, DIRS), F32),
        jax.ShapeDtypeStruct((1, DIRS), F32),
        jax.ShapeDtypeStruct(tile, F32),
        jax.ShapeDtypeStruct((2 * LAYERS, 8, 128), F32),
    )
    outs = pl.pallas_call(
        functools.partial(kernel, size, segs, cells),
        out_shape=tuple(pltpu.VMEM(s.shape, F32) for s in shapes),
        in_specs=[pl.BlockSpec(memory_space=pltpu.SMEM)] + [hbm] * 5,
        out_specs=(vmem,) * 5,
        scratch_shapes=[
            pltpu.VMEM((FIELDS, *tile), F32),
            pltpu.VMEM((FIELDS, *tile), F32),
            pltpu.VMEM((FIELDS, *tile), F32),
            pltpu.VMEM((2, FIELDS, BLOCKS, 8, 128), F32),
            pltpu.VMEM((2, FIELDS, BLOCKS, 8, 128), F32),
            pltpu.VMEM((2, 7, *tile), F32),
            pltpu.VMEM((3, *tile), F32),
            pltpu.VMEM(tile, F32),
            pltpu.VMEM(tile, F32),
            pltpu.VMEM((DIRS, 128), F32),
            pltpu.VMEM((count + 1, 2, 128), F32),
            pltpu.VMEM((peers, 2, 128), F32),
            pltpu.VMEM((count + 1, 1, 128), F32),
            pltpu.VMEM((peers, 1, 128), F32),
            pltpu.VMEM((DIRS, DIRS, 128), F32),
            pltpu.VMEM((DIRS, 128), F32),
            pltpu.VMEM((DIRS, DIRS, 128), F32),
            pltpu.VMEM((DIRS, DIRS, 8, 128), F32),
            pltpu.VMEM((DIRS, 8, 128), F32),
            pltpu.VMEM((4, 2 * LAYERS, 8, 128), F32),
            pltpu.VMEM((3, 2 * LAYERS, 8, 128), F32),
            dma((5,)),
            dma((2, F_GROUPS + 1)), dma((2, F_GROUPS + 1)), dma((2, G_GROUPS + 1)), dma((2, G_GROUPS + 1)),
            dma((peers,)), dma((peers,)), dma((peers,)), dma((peers,)),
            dma((3,)), dma((3,)),
        ],
        compiler_params=pltpu.CompilerParams(
            collective_id=0, has_side_effects=True, vmem_limit_bytes=40 * 1024 * 1024
        ),
        cost_estimate=pl.CostEstimate(flops=120_000_000, bytes_accessed=5_200_000, transcendentals=64),
        name="shadowing",
    )(
        segment_start,
        in_hbm(directions.reshape(DIRS, *tile)),
        in_hbm(adjoint.reshape(tile)),
        in_hbm(velocity.reshape(3, *tile)),
        in_hbm(diffusivity.reshape(tile)),
        in_hbm(objective_source.reshape(tile)),
    )
    basis_rows, upper, coefficients, shadow, gradient = pl.pallas_call(
        store_kernel,
        out_shape=shapes,
        in_specs=[pl.BlockSpec(memory_space=pl.ANY)] * 5,
        out_specs=(hbm,) * 5,
        scratch_shapes=[dma((STORES + 4,))],
        compiler_params=pltpu.CompilerParams(vmem_limit_bytes=1024 * 1024),
        name="store",
    )(*map(in_vmem, outs))
    return (
        basis_rows.reshape(directions.shape),
        upper[None],
        coefficients,
        shadow.reshape(adjoint.shape),
        gradient.reshape(LAYERS, 16, 128),
    )


def solution(mesh):
    return jax.shard_map(
        body,
        mesh=mesh,
        in_specs=(
            P("seg", None, "space", None, None),
            P("seg", "space", None, None),
            P("seg", None, "space", None, None),
            P("seg", "space", None, None),
            P("seg", "space", None, None),
            P("seg"),
        ),
        out_specs=(
            P("seg", None, "space", None, None),
            P("seg", None, None),
            P("seg", None),
            P("seg", "space", None, None),
            P("space", "seg", None),
        ),
        check_vma=False,
    )
```

```python
import functools
import math

import jax
import jax.numpy as jnp
from jax import lax
from jax.experimental import pallas as pl
from jax.experimental.pallas import tpu as pltpu
from jax.sharding import PartitionSpec as P

MESH = pl.DeviceIdType.MESH
DIRS = 16
FIELDS = 17
F_SIZE, G_SIZE = 4, 2
F_GROUPS, G_GROUPS = DIRS // F_SIZE, DIRS // G_SIZE
LAYERS = 4
STORES = 1
BLOCKS = 8
POS = LAYERS * BLOCKS
F32 = jnp.float32


def place_of(size):
    depth = min(4, size)
    width = min(4, size // depth)
    height = size // (depth * width)
    return height, width, depth


def peers_of(me, size):
    height, width, depth = place_of(size)
    z = lax.rem(me, depth)
    x = lax.rem(lax.div(me, depth), width)
    y = lax.div(me, depth * width)
    stages = [
        [
            ((y + 1 - 2 * lax.rem(y, 2) if a else y) * width + lax.rem(x + b, width)) * depth + z
            for a, b in ((1, 2), (1, 1), (1, 3), (0, 2), (1, 0), (0, 1), (0, 3))
        ],
        [
            ((height - 1 - y if a else y) * width + x) * depth + lax.rem(z + d, depth)
            for a, d in ((1, 1), (1, 3), (1, 2), (0, 1), (0, 3), (0, 2), (1, 0))
        ],
    ]
    return [stage for stage in stages if stage]


def layer(ref, lead, x):
    return ref[(*lead, pl.ds(BLOCKS * x, BLOCKS))].reshape(BLOCKS * 8, 128)


def stencil(here, ahead, behind, coef, step, x):
    c = [layer(coef, (step, n), x) for n in range(7)]
    out = c[0] * here + c[1] * ahead + c[2] * behind
    out = out + c[3] * pltpu.roll(here, BLOCKS * 8 - 1, 0) + c[4] * pltpu.roll(here, 1, 0)
    return out + c[5] * pltpu.roll(here, 127, 1) + c[6] * pltpu.roll(here, 1, 1)


def kernel(
    size, segs, cells,
    start_ref, dirs_ref, adj_ref, vel_ref, dif_ref, src_ref,
    basis_ref, upper_ref, coef_ref, shadow_ref, grad_ref,
    f_all, g_all, w_all, f_halo, g_halo, coef, vel, dif, src,
    gram, gram_cur, gram_got, along_cur, along_got, columns, inverse_rows, spread, inverse, weights, terms, arrived,
    load_sem, f_send, f_recv, g_send, g_recv,
    gram_send, gram_recv, along_send, along_recv, term_send, term_recv,
):
    seg = lax.axis_index("seg")
    me = lax.axis_index("space")
    right, left = lax.rem(me + 1, size), lax.rem(me + size - 1, size)
    stages = peers_of(me, size)

    barrier = pltpu.get_barrier_semaphore()
    greeted = [{"space": left}, {"space": right}]
    partners = [lax.rem(seg + 2, segs), segs - 1 - seg, seg + 1 - 2 * lax.rem(seg, 2)]
    greeted += [{"seg": partner} for partner in partners]
    greeted += [{"space": peer} for stage in reversed(stages) for peer in stage]
    for device in greeted:
        pl.semaphore_signal(barrier, inc=1, device_id=device, device_id_type=MESH)

    loads = [
        pltpu.make_async_copy(dirs_ref, f_all.at[pl.ds(0, DIRS)], load_sem.at[0]),
        pltpu.make_async_copy(adj_ref, f_all.at[DIRS], load_sem.at[1]),
        pltpu.make_async_copy(vel_ref, vel, load_sem.at[2]),
        pltpu.make_async_copy(dif_ref, dif, load_sem.at[3]),
        pltpu.make_async_copy(src_ref, src, load_sem.at[4]),
    ]
    for load in loads:
        load.start()

    def clear(n, _):
        w_all[n] = jnp.zeros((POS, 8, 128), F32)
        return 0

    lax.fori_loop(0, FIELDS, clear, 0)
    gram[...] = jnp.zeros_like(gram)
    for load in loads:
        load.wait()
    pl.semaphore_wait(barrier, len(greeted))

    def halo(source, landing, send, recv, n, side):
        return pltpu.make_async_remote_copy(
            source,
            landing,
            send.at[side, n],
            recv.at[side, n],
            device_id={"space": right if side == 0 else left},
            device_id_type=MESH,
        )

    edges = (pl.ds(BLOCKS * (LAYERS - 1), BLOCKS), pl.ds(0, BLOCKS))

    def f_copy(n, side):
        if n is F_GROUPS:
            return halo(f_all.at[DIRS, edges[side]], f_halo.at[side, DIRS], f_send, f_recv, n, side)
        fields = pl.ds(F_SIZE * n, F_SIZE)
        return halo(f_all.at[fields, edges[side]], f_halo.at[side, fields], f_send, f_recv, n, side)

    def g_copy(n, side):
        fields = DIRS if n is G_GROUPS else pl.ds(G_SIZE * n, G_SIZE)
        return halo(g_all.at[fields, edges[side]], g_halo.at[side, fields], g_send, g_recv, n, side)

    def begin(n, _):
        for side in range(2):
            f_copy(n, side).start()
        return 0

    lax.fori_loop(0, F_GROUPS, begin, 0)
    begin(F_GROUPS, 0)

    row = lax.broadcasted_iota(jnp.int32, (BLOCKS * 8, 128), 0)
    for step in range(2):
        phase = jnp.full((8, 128), start_ref[0], jnp.int32) + (1 - step)
        turn = lax.rem(phase, jnp.full((8, 128), 64, jnp.int32)).astype(F32)
        half = 0.5 * (1.0 + 0.5 * jnp.sin(2.0 * math.pi * turn / 64.0))
        half = jnp.broadcast_to(half[0:1], (BLOCKS * 8, 128))

        def prepare(x, _, step=step, half=half):
            spot = pl.ds(BLOCKS * x, BLOCKS)
            d = layer(dif, (), x)
            values = [1.0 - 6.0 * d]
            for axis in range(3):
                drift = half * layer(vel, (axis,), x)
                values += [d + drift, d - drift]
            values[3] = jnp.where(row == BLOCKS * 8 - 1, 0.0, values[3])
            values[4] = jnp.where(row == 0, 0.0, values[4])
            for n in range(7):
                coef[step, n, spot] = values[n].reshape(BLOCKS, 8, 128)
            return 0

        lax.fori_loop(0, LAYERS, prepare, 0)

    def advance(step, source, landing, target, n, layers):
        for x in layers:
            here = layer(source, (n,), x)
            ahead = layer(source, (n,), x + 1) if x < LAYERS - 1 else landing[1, n].reshape(BLOCKS * 8, 128)
            behind = layer(source, (n,), x - 1) if x > 0 else landing[0, n].reshape(BLOCKS * 8, 128)
            out = stencil(here, ahead, behind, coef, step, x)
            target[n, pl.ds(BLOCKS * x, BLOCKS)] = out.reshape(BLOCKS, 8, 128)

        @pl.when(n == DIRS)
        def _():
            for x in layers:
                spot = pl.ds(BLOCKS * x, BLOCKS)
                target[n, spot] = target[n, spot] + src[spot]

    def each(p, work):
        def one(n, _):
            work(n)
            return 0

        lax.fori_loop(G_SIZE * p, jnp.minimum(G_SIZE * (p + 1), FIELDS), one, 0)

    def either(p, work):
        pl.when(p < G_GROUPS)(lambda: work(p))
        pl.when(p == G_GROUPS)(lambda: work(G_GROUPS))

    def both_sides(action):
        for side in range(2):
            action(side)

    ratio = F_SIZE // G_SIZE

    def first(p, _):
        @pl.when(jnp.logical_and(p < G_GROUPS, lax.rem(p, ratio) == 0))
        def _():
            both_sides(lambda side: f_copy(lax.div(p, ratio), side).wait_recv())

        @pl.when(p == G_GROUPS)
        def _():
            both_sides(lambda side: f_copy(F_GROUPS, side).wait_recv())

        each(p, lambda n: advance(0, f_all, f_halo, g_all, n, (0, 3)))
        either(p, lambda group: both_sides(lambda side: g_copy(group, side).start()))
        each(p, lambda n: advance(0, f_all, f_halo, g_all, n, (1, 2)))
        return 0

    lax.fori_loop(0, G_GROUPS + 1, first, 0)

    lane = lax.broadcasted_iota(jnp.int32, (DIRS, 128), 1)

    def exchange(cur, got, send, recv, k):
        base = sum(len(stage) for stage in stages[:k])
        return [
            pltpu.make_async_remote_copy(
                cur.at[k], got.at[base + n], send.at[base + n], recv.at[base + n],
                device_id={"space": peer}, device_id_type=MESH,
            )
            for n, peer in enumerate(stages[k])
        ]

    gram_parts = functools.partial(exchange, gram_cur, gram_got, gram_send, gram_recv)
    along_parts = functools.partial(exchange, along_cur, along_got, along_send, along_recv)

    def collect(parts, cur, got, k):
        base = sum(len(stage) for stage in stages[:k])
        for copy in parts(k):
            copy.wait_recv()
        total = cur[k]
        for n in range(len(stages[k])):
            total = total + got[base + n]
        cur[k + 1] = total

    sublane = lax.broadcasted_iota(jnp.int32, (DIRS, 128), 0)
    diagonal = lane == sublane
    group_of = lane // DIRS == sublane % 8
    def gram_row(n):
        def at(p, total):
            return total + w_all[0:DIRS, p] * w_all[n, p][None]

        total = lax.fori_loop(0, POS, at, jnp.zeros((DIRS, 8, 128), F32), unroll=4)
        column = jnp.sum(jnp.sum(total, axis=1), axis=1, keepdims=True)
        gram[...] = jnp.where(lane == n, column, gram[...])

    def second(p, _):
        @pl.when(p == G_GROUPS)
        def _():
            packed = pltpu.roll(gram[...], 0, 1, stride=DIRS, stride_axis=0)
            for h in range(2):
                gram_cur[0, h:h + 1, :] = jnp.sum(packed[8 * h:8 * h + 8], axis=0, keepdims=True)
            for copy in gram_parts(0):
                copy.start()

        each(p, lambda n: advance(1, g_all, g_halo, w_all, n, (1, 2)))
        either(p, lambda group: both_sides(lambda side: g_copy(group, side).wait_recv()))
        each(p, lambda n: advance(1, g_all, g_halo, w_all, n, (0, 3)))
        each(p, gram_row)
        return 0

    lax.fori_loop(0, G_GROUPS + 1, second, 0)
    along_column = jnp.broadcast_to(gram[:, DIRS:DIRS + 1], (DIRS, 128))
    along_cur[0] = jnp.sum(jnp.where(diagonal, along_column, 0.0), axis=0, keepdims=True)
    for copy in along_parts(0):
        copy.start()
    count = len(stages)
    for k in range(count):
        collect(gram_parts, gram_cur, gram_got, k)
        if k + 1 < count:
            for copy in gram_parts(k + 1):
                copy.start()
            collect(along_parts, along_cur, along_got, k)
            for copy in along_parts(k + 1):
                copy.start()

    packed = jnp.concatenate(
        [jnp.broadcast_to(gram_cur[count, h:h + 1, :], (8, 128)) for h in range(2)], axis=0
    )
    whole = jnp.where(group_of, packed * (1.0 / cells), 0.0)
    for bit in (1, 2, 4):
        moved = pltpu.roll(whole, 128 - DIRS * bit, 1)
        whole = jnp.where(lax.rem(sublane // bit, 2) == 1, moved, whole)
    for j in range(DIRS):
        columns[j] = jnp.broadcast_to(whole[:, j:j + 1], (DIRS, 128))
    lane8 = lax.broadcasted_iota(jnp.int32, (8, 128), 1)
    cols = [jnp.broadcast_to(columns[k:DIRS, k:k + 1, :], (DIRS - k, 8, 128)) for k in range(DIRS)]
    rows = [
        jnp.broadcast_to(whole[i:i + 1], (8, 128)) + jnp.where(lane8 == 32 + i, 1.0, 0.0) for i in range(DIRS)
    ]
    for k in range(DIRS):
        scale = lax.rsqrt(cols[k][0])
        lower = cols[k] * scale[None]
        done = rows[k] * scale
        inverse_rows[k:k + 1, :] = done[0:1]
        for j in range(k + 1, DIRS):
            cols[j] = cols[j] - lower[j - k:] * lower[j - k][None]
            rows[j] = rows[j] - lower[j - k] * done
    solved = inverse_rows[...]
    for k in range(DIRS):
        spread[k] = jnp.broadcast_to(solved[:, 32 + k:33 + k], (DIRS, 128))

    collect(along_parts, along_cur, along_got, count - 1)
    along = along_cur[count] * (1.0 / cells)
    shifted = pltpu.roll(solved, 96, 1)
    found = jnp.sum(shifted * along, axis=1, keepdims=True)
    weight_row = jnp.sum(shifted * found, axis=0, keepdims=True)
    for k in range(DIRS):
        weights[k] = jnp.broadcast_to(weight_row[:, k:k + 1], (8, 128))

    def piece(t):
        for x in range(LAYERS):
            for h in range(2):
                p = BLOCKS * x + 2 * t + h
                value = w_all[DIRS, p]
                for k in range(DIRS):
                    value = value - weights[k] * w_all[k, p]
                shadow_ref[p] = value
                terms[t, 2 * x + h] = value + g_all[DIRS, p]

    term_copies = [
        pltpu.make_async_remote_copy(
            terms.at[partner], arrived.at[n], term_send.at[n], term_recv.at[n],
            device_id={"seg": partner}, device_id_type=MESH,
        )
        for n, partner in enumerate(partners)
    ]
    for partner, copy in zip(partners, term_copies):
        piece(partner)
        copy.start()
    piece(seg)

    upper_ref[...] = jnp.where(lane >= sublane, solved, 0.0)[:, 0:DIRS]
    coef_ref[...] = jnp.sum(jnp.where(diagonal, found, 0.0), axis=0, keepdims=True)[:, 0:DIRS]

    for k in range(DIRS):
        for i in range(k, DIRS):
            inverse[i, k] = jnp.broadcast_to(spread[k, i:i + 1, :], (8, 128))

    def rows_at(q, _):
        spot = pl.ds(2 * q, 2)
        values = [w_all[k, spot] for k in range(DIRS)]
        for i in range(DIRS):
            total = inverse[i, 0][None] * values[0]
            for k in range(1, i + 1):
                total = total + inverse[i, k][None] * values[k]
            basis_ref[i, spot] = total
        return 0

    lax.fori_loop(0, POS // 2, rows_at, 0)

    def sent_f(n, _):
        for side in range(2):
            f_copy(n, side).wait_send()
        return 0

    def sent_g(n, _):
        for side in range(2):
            g_copy(n, side).wait_send()
        return 0

    lax.fori_loop(0, F_GROUPS, sent_f, 0)
    sent_f(F_GROUPS, 0)
    lax.fori_loop(0, G_GROUPS, sent_g, 0)
    sent_g(G_GROUPS, 0)
    for k in range(count):
        for copy in gram_parts(k) + along_parts(k):
            copy.wait_send()
    for copy in term_copies:
        copy.wait_recv()
    grad_ref[...] = terms[seg] + arrived[0] + arrived[1] + arrived[2]
    for copy in term_copies:
        copy.wait_send()


def in_hbm(array):
    return pltpu.with_memory_space_constraint(array, pltpu.HBM)


def in_vmem(array):
    return pltpu.with_memory_space_constraint(array, pltpu.VMEM)


def store_kernel(*refs):
    held, out, sems = refs[:5], refs[5:10], refs[10]
    part = DIRS // STORES
    copies = [
        pltpu.make_async_copy(held[0].at[pl.ds(part * n, part)], out[0].at[pl.ds(part * n, part)], sems.at[n])
        for n in range(STORES)
    ]
    copies += [pltpu.make_async_copy(held[n], out[n], sems.at[STORES + n - 1]) for n in range(1, 5)]
    for copy in copies:
        copy.start()
    for copy in copies:
        copy.wait()


def body(directions, adjoint, velocity, diffusivity, objective_source, segment_start):
    size, segs = lax.axis_size("space"), lax.axis_size("seg")
    tile = (POS, 8, 128)
    cells = POS * 8 * 128 * size
    height, width, depth = place_of(size)
    groups = [8, 8]
    peers, count = sum(groups) - len(groups), len(groups)
    hbm, vmem = pl.BlockSpec(memory_space=pltpu.HBM), pl.BlockSpec(memory_space=pltpu.VMEM)
    dma = pltpu.SemaphoreType.DMA
    shapes = (
        jax.ShapeDtypeStruct((DIRS, *tile), F32),
        jax.ShapeDtypeStruct((DIRS, DIRS), F32),
        jax.ShapeDtypeStruct((1, DIRS), F32),
        jax.ShapeDtypeStruct(tile, F32),
        jax.ShapeDtypeStruct((2 * LAYERS, 8, 128), F32),
    )
    outs = pl.pallas_call(
        functools.partial(kernel, size, segs, cells),
        out_shape=tuple(pltpu.VMEM(s.shape, F32) for s in shapes),
        in_specs=[pl.BlockSpec(memory_space=pltpu.SMEM)] + [hbm] * 5,
        out_specs=(vmem,) * 5,
        scratch_shapes=[
            pltpu.VMEM((FIELDS, *tile), F32),
            pltpu.VMEM((FIELDS, *tile), F32),
            pltpu.VMEM((FIELDS, *tile), F32),
            pltpu.VMEM((2, FIELDS, BLOCKS, 8, 128), F32),
            pltpu.VMEM((2, FIELDS, BLOCKS, 8, 128), F32),
            pltpu.VMEM((2, 7, *tile), F32),
            pltpu.VMEM((3, *tile), F32),
            pltpu.VMEM(tile, F32),
            pltpu.VMEM(tile, F32),
            pltpu.VMEM((DIRS, 128), F32),
            pltpu.VMEM((count + 1, 2, 128), F32),
            pltpu.VMEM((peers, 2, 128), F32),
            pltpu.VMEM((count + 1, 1, 128), F32),
            pltpu.VMEM((peers, 1, 128), F32),
            pltpu.VMEM((DIRS, DIRS, 128), F32),
            pltpu.VMEM((DIRS, 128), F32),
            pltpu.VMEM((DIRS, DIRS, 128), F32),
            pltpu.VMEM((DIRS, DIRS, 8, 128), F32),
            pltpu.VMEM((DIRS, 8, 128), F32),
            pltpu.VMEM((4, 2 * LAYERS, 8, 128), F32),
            pltpu.VMEM((3, 2 * LAYERS, 8, 128), F32),
            dma((5,)),
            dma((2, F_GROUPS + 1)), dma((2, F_GROUPS + 1)), dma((2, G_GROUPS + 1)), dma((2, G_GROUPS + 1)),
            dma((peers,)), dma((peers,)), dma((peers,)), dma((peers,)),
            dma((3,)), dma((3,)),
        ],
        compiler_params=pltpu.CompilerParams(
            collective_id=0, has_side_effects=True, vmem_limit_bytes=40 * 1024 * 1024
        ),
        cost_estimate=pl.CostEstimate(flops=120_000_000, bytes_accessed=5_200_000, transcendentals=64),
        name="shadowing",
    )(
        segment_start,
        in_hbm(directions.reshape(DIRS, *tile)),
        in_hbm(adjoint.reshape(tile)),
        in_hbm(velocity.reshape(3, *tile)),
        in_hbm(diffusivity.reshape(tile)),
        in_hbm(objective_source.reshape(tile)),
    )
    basis_rows, upper, coefficients, shadow, gradient = pl.pallas_call(
        store_kernel,
        out_shape=shapes,
        in_specs=[pl.BlockSpec(memory_space=pl.ANY)] * 5,
        out_specs=(hbm,) * 5,
        scratch_shapes=[dma((STORES + 4,))],
        compiler_params=pltpu.CompilerParams(vmem_limit_bytes=1024 * 1024),
        name="store",
    )(*map(in_vmem, outs))
    return (
        basis_rows.reshape(directions.shape),
        upper[None],
        coefficients,
        shadow.reshape(adjoint.shape),
        gradient.reshape(LAYERS, 16, 128),
    )


def solution(mesh):
    return jax.shard_map(
        body,
        mesh=mesh,
        in_specs=(
            P("seg", None, "space", None, None),
            P("seg", "space", None, None),
            P("seg", None, "space", None, None),
            P("seg", "space", None, None),
            P("seg", "space", None, None),
            P("seg"),
        ),
        out_specs=(
            P("seg", None, "space", None, None),
            P("seg", None, None),
            P("seg", None),
            P("seg", "space", None, None),
            P("space", "seg", None),
        ),
        check_vma=False,
    )
```
